32 devices in a mesh: parts: 32 (over z, y, x, core).
Axes of the slice: x: 2, y: 2, z: 4, core: 2. Of those that a mesh axis runs over, the one named last changes fastest.
Arguments:
- flow_state: float32 [5, 64, 2048], P(None, None, 'parts'), may hold values from -2 to 14, as said below
- state_tangent: float32 [5, 64, 2048], P(None, None, 'parts'), may hold values from -6 to 6
- far_field: float32 [5], replicated, may hold values from -0.3 to 5, as said below
- coordinates: float32 [3, 3264], P(None, 'parts'), as said below
- damping: float32 [2], replicated, may hold values from 0.1 to 1
- face_neighbour: int32 [6, 2048], P(None, 'parts'), may hold values from 0 to 96, as said below
- element_nodes: int32 [8, 2048], P(None, 'parts'), may hold values from 0 to 152, as said below
- upper_sends: int32 [1024], P('parts'), may hold values from 0 to 63, as said below
- lower_sends: int32 [1024], P('parts'), may hold values from 0 to 63, as said below
- node_sends: int32 [1632], P('parts'), may hold values from 0 to 101, as said below
- shock_flags: int32 [2048], P('parts'), may hold values from 0 to 1, as said below
Outputs:
- residual: float32 [5, 64, 2048], P(None, None, 'parts')
- state_change: float32 [5, 64, 2048], P(None, None, 'parts')
- node_update: float32 [3, 3264], P(None, 'parts')
The draws below stay inside these ranges and needn't reach their ends.
Inputs may be any that keep to these rules, and one draw needn't show every extreme that they name: `flow_state`: density and pressure at each point lie in 0.5 to 2 and velocity components within 1 of (0, 0, 1.5). `far_field`: density and pressure lie in 0.8 to 1.2, velocity components within 0.2 of (0, 0, 1.5). `coordinates`: hexahedra stay valid: each element's trilinear map keeps a positive Jacobian at all points. `face_neighbour`: entry f of an element is a local element below 64, 64 + a halo slot below 32 (faces 0 and 1 only), or 96 for the far field; neighbours share the element's reference orientation. `element_nodes`: a local owned node below 102, or 102 + a halo slot of a node owned by the next partition. `upper_sends`: on each partition 32 distinct local elements. `lower_sends`: on each partition 32 distinct local elements. `node_sends`: on each partition 51 distinct owned nodes. `shock_flags`: at most 16 flagged elements in one partition, and some partition has exactly 16.
All inputs are finite; a program needn't handle non-finite values.
Results may differ from the reference program's by a relative error of at most 0.0003.
Values sent between devices are 32-bit elements; how exact they have to be, the bound alone decides.
A program may use at most 128 MiB of HBM per device.

```python
import math
import jax
import jax.numpy as jnp
import numpy as np
from jax import lax

NT = 2
NN = 16
NW = 2
VARS = 5
QPTS = 64
EL = 64
HS = 32
NE = 2048
NH = 51
NO = 102
NNODE = 3264
FLAG_MAX = 16
N_PARTS = 32


def partition_orders(key, salt, length):
    partitions = NE // EL
    keys = jax.random.split(jax.random.fold_in(key, salt), partitions)
    return jax.vmap(lambda k: jax.random.permutation(k, length))(keys)


def mesh_layout(key):
    partitions = NE // EL
    element_order = partition_orders(key, 101, EL)
    node_order = partition_orders(key, 102, NO)
    lower_slots = partition_orders(key, 103, HS)
    upper_slots = partition_orders(key, 104, HS)
    node_slots = partition_orders(key, 105, NH)
    return (partitions, element_order, node_order, lower_slots, upper_slots, node_slots)


def element_columns(partitions, element_order):
    return (jnp.arange(partitions, dtype=jnp.int32)[:, None] * EL + element_order).reshape(-1)


def draw_face_neighbour(key, part):
    partitions, element_order, node_order, lower_slots, upper_slots, node_slots = mesh_layout(key)
    canonical = jnp.arange(EL, dtype=jnp.int32)
    column = canonical // HS
    rest = canonical % HS
    along = rest // NN
    across = rest % NN
    outside = EL + HS

    def beside(offset):
        return jnp.take(element_order, jnp.clip(canonical + offset, 0, EL - 1), axis=1)
    entries = [jnp.where(column > 0, beside(-HS), EL + jnp.take(lower_slots, rest, axis=1)), jnp.where(column < NW - 1, beside(HS), EL + jnp.take(upper_slots, rest, axis=1)), jnp.where(along > 0, beside(-NN), outside), jnp.where(along < NT - 1, beside(NN), outside), jnp.where(across > 0, beside(-1), outside), jnp.where(across < NN - 1, beside(1), outside)]
    stacked = jnp.stack([jnp.broadcast_to(e, (partitions, EL)) for e in entries]).astype(jnp.int32)
    return jnp.zeros((6, NE), jnp.int32).at[:, element_columns(partitions, element_order)].set(stacked.reshape(6, -1))


def draw_element_nodes(key, part):
    partitions, element_order, node_order, lower_slots, upper_slots, node_slots = mesh_layout(key)
    canonical = jnp.arange(EL, dtype=jnp.int32)
    column = canonical // HS
    rest = canonical % HS
    along = rest // NN
    across = rest % NN
    entries = []
    for k in range(8):
        target = (along + k // 2 % 2) * (NN + 1) + across + k % 2
        node_column = column + k // 4
        local_node = jnp.take(node_order, jnp.minimum(node_column * NH + target, NO - 1), axis=1)
        halo_node = NO + jnp.take(node_slots, target, axis=1)
        entries.append(jnp.where(node_column < NW, local_node, halo_node))
    stacked = jnp.stack(entries).astype(jnp.int32)
    return jnp.zeros((8, NE), jnp.int32).at[:, element_columns(partitions, element_order)].set(stacked.reshape(8, -1))


def sends_from(partitions, receiver_slots, sender_values, length):
    columns = (jnp.arange(partitions, dtype=jnp.int32)[:, None] * length + receiver_slots).reshape(-1)
    return jnp.zeros((partitions * length,), jnp.int32).at[columns].set(sender_values.reshape(-1).astype(jnp.int32))


def draw_upper_sends(key, part):
    partitions, element_order, node_order, lower_slots, upper_slots, node_slots = mesh_layout(key)
    return sends_from(partitions, jnp.roll(lower_slots, -1, axis=0), element_order[:, (NW - 1) * HS:], HS)


def draw_lower_sends(key, part):
    partitions, element_order, node_order, lower_slots, upper_slots, node_slots = mesh_layout(key)
    return sends_from(partitions, jnp.roll(upper_slots, 1, axis=0), element_order[:, :HS], HS)


def draw_node_sends(key, part):
    partitions, element_order, node_order, lower_slots, upper_slots, node_slots = mesh_layout(key)
    return sends_from(partitions, jnp.roll(node_slots, 1, axis=0), node_order[:, :NH], NH)


def draw_coordinates(key, part):
    partitions, element_order, node_order, lower_slots, upper_slots, node_slots = mesh_layout(key)
    canonical = jnp.arange(NO)
    column = (canonical // NH).astype(jnp.float32)
    rest = canonical % NH
    along = (rest // (NN + 1)).astype(jnp.float32)
    across = (rest % (NN + 1)).astype(jnp.float32)
    azimuth = 2.0 * math.pi / (partitions * NW) * (NW * jnp.arange(partitions, dtype=jnp.float32)[:, None] + column[None, :])
    radius = partitions * NW / (2.0 * math.pi) + 0.6 * across
    jitter_key = jax.random.fold_in(key, 106)
    jitter = 0.04 * jax.random.truncated_normal(jitter_key, -2.0, 2.0, (3, partitions, NO), jnp.float32)
    positions = jnp.stack([radius * jnp.cos(azimuth) + jitter[0], radius * jnp.sin(azimuth) + jitter[1], jnp.broadcast_to(along, (partitions, NO)) + jitter[2]])
    columns = (jnp.arange(partitions, dtype=jnp.int32)[:, None] * NO + node_order).reshape(-1)
    return jnp.zeros((3, NNODE), jnp.float32).at[:, columns].set(positions.reshape(3, -1))


def draw_shock_flags(key, part):
    partitions = NE // EL
    ranks = partition_orders(key, 107, EL)
    indices = jnp.arange(partitions, dtype=jnp.int32)
    lowest = FLAG_MAX * (partitions + 2 * indices) // (3 * partitions)
    counts = jax.random.randint(jax.random.fold_in(key, 108), (partitions,), lowest, FLAG_MAX + 1)
    fullest = jax.random.randint(jax.random.fold_in(key, 109), (), 0, partitions)
    counts = jnp.where(indices == fullest, FLAG_MAX, counts)
    return (ranks < counts[:, None]).astype(jnp.int32).reshape(-1)


def conserved(density, velocity, pressure):
    energy = pressure / 0.4 + 0.5 * density * jnp.sum(velocity * velocity, axis=0)
    return jnp.concatenate([density[None], density[None] * velocity, energy[None]], axis=0)


def draw_flow_state(key, part):
    keys = jax.random.split(jax.random.fold_in(key, 201), 3)
    point_shape = (64, NE)
    density = jnp.exp(jax.random.uniform(keys[0], point_shape, jnp.float32, math.log(0.5), math.log(2.0)))
    pressure = jnp.exp(jax.random.uniform(keys[1], point_shape, jnp.float32, math.log(0.5), math.log(2.0)))
    velocity = jnp.clip(0.5 * jax.random.normal(keys[2], (3,) + point_shape, jnp.float32), -1.0, 1.0)
    velocity = velocity + jnp.array([0.0, 0.0, 1.5], jnp.float32).reshape(3, 1, 1)
    return conserved(density, velocity, pressure)


def draw_far_field(key, part):
    keys = jax.random.split(jax.random.fold_in(key, 301), 3)
    density = jax.random.uniform(keys[0], (1,), jnp.float32, 0.8, 1.2)
    pressure = jax.random.uniform(keys[1], (1,), jnp.float32, 0.8, 1.2)
    velocity = jax.random.uniform(keys[2], (3, 1), jnp.float32, -0.2, 0.2) + jnp.array([0.0, 0.0, 1.5], jnp.float32).reshape(3, 1)
    return conserved(density, velocity, pressure).reshape(5)


def levels(own_key, extent, shards, least, high):
    def one(axis_at, shards_of):
        draws = jax.random.uniform(jax.random.fold_in(jax.random.fold_in(own_key, 6), axis_at), (shards_of,), jnp.float32, least / len(shards), high / len(shards))
        return jnp.repeat(jnp.exp(draws), extent[axis_at] // shards_of).reshape((-1,) + (1,) * (len(extent) - axis_at - 1))

    loudness = one(*shards[0])
    for cut in shards[1:]:
        loudness = loudness * one(*cut)
    return loudness


def noise(rng, dims, spread, bound, cuts=(), kind=jnp.bfloat16):
    values = jax.random.normal(rng, dims, jnp.float32) * spread
    if len(cuts) > 0:
        values = levels(rng, dims, cuts, -0.22, 0.18) * values
    return jnp.clip(values, min=-bound, max=bound).astype(kind)


def setup_inputs(seed: int = 0) -> dict:
    splits = jax.random.split(jax.random.key(seed), 12)
    return {
        "flow_state": draw_flow_state(jax.random.fold_in(splits[11], 71), 0),
        "state_tangent": noise(splits[1], (VARS, QPTS, NE), 1.0, 6.0, ((2, 32),), jnp.float32),
        "far_field": draw_far_field(jax.random.fold_in(splits[11], 71), 0),
        "coordinates": draw_coordinates(jax.random.fold_in(splits[11], 71), 0),
        "damping": jnp.clip(jnp.exp(jax.random.uniform(splits[4], (2,), jnp.float32, math.log(0.1), math.log(1.0))), 0.1, 1.0),
        "face_neighbour": draw_face_neighbour(jax.random.fold_in(splits[11], 71), 0),
        "element_nodes": draw_element_nodes(jax.random.fold_in(splits[11], 71), 0),
        "upper_sends": draw_upper_sends(jax.random.fold_in(splits[11], 71), 0),
        "lower_sends": draw_lower_sends(jax.random.fold_in(splits[11], 71), 0),
        "node_sends": draw_node_sends(jax.random.fold_in(splits[11], 71), 0),
        "shock_flags": draw_shock_flags(jax.random.fold_in(splits[11], 71), 0),
    }


GAMMA = 1.4
SOFTENING = 0.01
HIGHEST = lax.Precision.HIGHEST

def lobatto_tables():
    points = np.array([-1.0, -math.sqrt(0.2), math.sqrt(0.2), 1.0])
    weights = np.array([1.0, 5.0, 5.0, 1.0]) / 6.0
    derivative = np.zeros((4, 4))
    for a in range(4):
        for b in range(4):
            if a == b:
                derivative[a, b] = sum((1.0 / (points[a] - points[m]) for m in range(4) if m != a))
            else:
                numerator = 1.0
                denominator = 1.0
                for m in range(4):
                    if m != b:
                        denominator *= points[b] - points[m]
                        if m != a:
                            numerator *= points[a] - points[m]
                derivative[a, b] = numerator / denominator
    return (points, weights, derivative)

def shape_gradients():
    points = lobatto_tables()[0]
    gradients = np.zeros((3, 64, 8))
    for q in range(64):
        position = (q // 16, q // 4 % 4, q % 4)
        for k in range(8):
            corner_bits = (k // 4, k // 2 % 2, k % 2)
            for j in range(3):
                factor = 1.0
                for m in range(3):
                    orient = 1.0 if corner_bits[m] == 1 else -1.0
                    if m == j:
                        factor *= 0.5 * orient
                    else:
                        factor *= 0.5 * (1.0 + orient * points[position[m]])
                gradients[j, q, k] = factor
    return gradients

def edge_laplacian():
    matrix = np.zeros((8, 8))
    for k in range(8):
        matrix[k, k] = 3.0
        for b in range(3):
            matrix[k, k ^ 1 << b] = -1.0
    return matrix

def area_vectors(corners):
    gradients = jnp.asarray(shape_gradients(), jnp.float32)
    tangents = [[jnp.dot(gradients[j], corners[i], precision=HIGHEST, preferred_element_type=jnp.float32) for i in range(3)] for j in range(3)]
    result = []
    for j in range(3):
        first_edge = tangents[(j + 1) % 3]
        second = tangents[(j + 2) % 3]
        result.append(jnp.stack([first_edge[1] * second[2] - first_edge[2] * second[1], first_edge[2] * second[0] - first_edge[0] * second[2], first_edge[0] * second[1] - first_edge[1] * second[0]]))
    return result

def euler_flux(values):
    density = values[0]
    momentum = values[1:4]
    energy = values[4]
    velocity = momentum / density
    pressure = (GAMMA - 1.0) * (energy - 0.5 * lax.optimization_barrier(jnp.sum(momentum * velocity, axis=0)))
    fluxes = []
    for i in range(3):
        components = [momentum[i]]
        for m in range(3):
            component = momentum[m] * velocity[i]
            if m == i:
                component = component + pressure
            components.append(component)
        components.append((energy + pressure) * velocity[i])
        fluxes.append(jnp.stack(components))
    return (fluxes, velocity, pressure)

def numerical_flux(inner_face, outer_face, normal):
    inner_fluxes, inner_velocity, inner_pressure = euler_flux(inner_face)
    outer_fluxes, outer_velocity, outer_pressure = euler_flux(outer_face)
    inner_normal = sum((normal[i] * inner_fluxes[i] for i in range(3)))
    outer_normal = sum((normal[i] * outer_fluxes[i] for i in range(3)))
    area_square = lax.optimization_barrier(jnp.sum(normal * normal, axis=0))
    area_size = jnp.sqrt(area_square)
    inner_along = lax.optimization_barrier(jnp.sum(inner_velocity * normal, axis=0))
    outer_along = lax.optimization_barrier(jnp.sum(outer_velocity * normal, axis=0))
    inner_speed = jnp.sqrt(inner_along * inner_along + SOFTENING * area_square) + jnp.sqrt(GAMMA * inner_pressure / inner_face[0]) * area_size
    outer_speed = jnp.sqrt(outer_along * outer_along + SOFTENING * area_square) + jnp.sqrt(GAMMA * outer_pressure / outer_face[0]) * area_size
    difference = inner_speed - outer_speed
    wave_speed = 0.5 * (inner_speed + outer_speed) + 0.5 * jnp.sqrt(difference * difference + SOFTENING * area_square)
    common = 0.5 * (inner_normal + outer_normal) - 0.5 * wave_speed * (outer_face - inner_face)
    return common - inner_normal

def element_residual(values, neighbours, corners):
    points, weights, derivative = lobatto_tables()
    derivative = jnp.asarray(derivative, jnp.float32)
    volume_weights = jnp.asarray(weights[:, None, None] * weights[None, :, None] * weights[None, None, :], jnp.float32)
    face_weights = jnp.asarray(weights[:, None] * weights[None, :], jnp.float32).reshape(1, 16, 1)
    columns = values.shape[-1]
    normals = area_vectors(corners)
    fluxes = euler_flux(values)[0]
    patterns = ['ab,vbcde->vacde', 'ab,vcbde->vcade', 'ab,vcdbe->vcdae']
    divergence = jnp.zeros((5, 4, 4, 4, columns), jnp.float32)
    for j in range(3):
        contravariant = sum((normals[j][i] * fluxes[i] for i in range(3))).reshape(5, 4, 4, 4, columns)
        divergence = divergence + jnp.einsum(patterns[j], derivative, contravariant, precision=HIGHEST)
    result = divergence * volume_weights[None, :, :, :, None]
    reshaped = values.reshape(5, 4, 4, 4, columns)
    for f in range(6):
        j = f // 2
        face_side = f % 2
        inner_face = lax.index_in_dim(reshaped, 3 * face_side, axis=1 + j, keepdims=False).reshape(5, 16, columns)
        normal = lax.index_in_dim(normals[j].reshape(3, 4, 4, 4, columns), 3 * face_side, axis=1 + j, keepdims=False).reshape(3, 16, columns) * (2.0 * face_side - 1.0)
        jump_term = numerical_flux(inner_face, neighbours[f], normal) * face_weights
        location = (slice(None),) * (1 + j) + (3 * face_side,)
        result = result.at[location].add(jump_term.reshape(5, 4, 4, columns))
    return result.reshape(5, 64, columns)

def face_traces(values):
    columns = values.shape[-1]
    reshaped = values.reshape(5, 4, 4, 4, columns)
    return [lax.index_in_dim(reshaped, 3 * (f % 2), axis=1 + f // 2, keepdims=False).reshape(5, 16, columns) for f in range(6)]

def neighbour_states(traces, lower_halo, upper_halo, far_field, face_neighbour):
    outer_cell = jnp.broadcast_to(far_field.reshape(5, 1, 1), (5, 16, 1))
    empty_block = jnp.zeros_like(lower_halo)
    result = []
    for f in range(6):
        halo_part = lower_halo if f == 0 else upper_halo if f == 1 else empty_block
        lookup_table = jnp.concatenate([traces[f ^ 1], halo_part, outer_cell], axis=2)
        result.append(jnp.take(lookup_table, face_neighbour[f], axis=2))
    return result

def partition_major(array, partitions):
    array_shape = array.shape
    return jnp.moveaxis(array.reshape(array_shape[:-1] + (partitions, array_shape[-1] // partitions)), -2, 0)

def partition_minor(array):
    return jnp.moveaxis(array, 0, -2).reshape(array.shape[1:-1] + (-1,))

def reference(flow_state, state_tangent, far_field, coordinates, damping, face_neighbour, element_nodes, upper_sends, lower_sends, node_sends, shock_flags):
    partitions = N_PARTS
    states = partition_major(flow_state, partitions)
    tangents = partition_major(state_tangent, partitions)
    neighbour_lists = partition_major(face_neighbour, partitions)
    corner_lists = partition_major(element_nodes, partitions)
    upper_lists = partition_major(upper_sends, partitions)
    lower_lists = partition_major(lower_sends, partitions)
    node_lists = partition_major(node_sends, partitions)
    flag_rows = partition_major(shock_flags, partitions)
    places = partition_major(coordinates, partitions)
    strength = damping[0]
    smoothing = damping[1]
    laplacian = jnp.asarray(edge_laplacian(), jnp.float32)
    node_count = places.shape[2]
    halo_count = node_lists.shape[1]

    def outgoing(items):
        values, tangent, upper_list, lower_list, node_list, place = items
        traces = face_traces(values)
        tangent_traces = face_traces(tangent)
        return (jnp.take(traces[1], upper_list, axis=2), jnp.take(tangent_traces[1], upper_list, axis=2), jnp.take(traces[0], lower_list, axis=2), jnp.take(tangent_traces[0], lower_list, axis=2), jnp.take(place, node_list, axis=1))
    sent = lax.map(outgoing, (states, tangents, upper_lists, lower_lists, node_lists, places))
    lower_halos = jnp.roll(sent[0], 1, axis=0)
    lower_tangents = jnp.roll(sent[1], 1, axis=0)
    upper_halos = jnp.roll(sent[2], -1, axis=0)
    upper_tangents = jnp.roll(sent[3], -1, axis=0)
    halo_places = jnp.roll(sent[4], -1, axis=0)

    def first_pass(items):
        values, tangent, lower_halo, lower_tangent, upper_halo, upper_tangent, neighbour_list, corner_list, place, halo_place, flag_row = items
        outer_states = neighbour_states(face_traces(values), lower_halo, upper_halo, far_field, neighbour_list)
        outer_tangents = neighbour_states(face_traces(tangent), lower_tangent, upper_tangent, jnp.zeros_like(far_field), neighbour_list)
        corners = jnp.take(jnp.concatenate([place, halo_place], axis=1), corner_list, axis=1)
        residual, change = jax.jvp(lambda v, o: element_residual(v, o, corners), (values, outer_states), (tangent, outer_tangents))
        weight = flag_row.astype(jnp.float32)
        pullback = jax.vjp(lambda c: element_residual(values, outer_states, c), corners)[1]
        corner_grad = pullback(residual * weight)[0]
        corner_grad = corner_grad + smoothing * weight * jnp.einsum('ike,kl->ile', corners, laplacian, precision=HIGHEST)
        grad_table = jnp.zeros((3, node_count + halo_count), jnp.float32).at[:, corner_list].add(corner_grad)
        count_table = jnp.zeros((node_count + halo_count,), jnp.float32).at[corner_list].add(jnp.broadcast_to(weight, corner_list.shape))
        return (residual, change, grad_table, count_table)
    residuals, changes, grad_tables, count_tables = lax.map(first_pass, (states, tangents, lower_halos, lower_tangents, upper_halos, upper_tangents, neighbour_lists, corner_lists, places, halo_places, flag_rows))
    back_grads = jnp.roll(grad_tables[:, :, node_count:], 1, axis=0)
    back_counts = jnp.roll(count_tables[:, node_count:], 1, axis=0)

    def assemble(items):
        grad_table, count_table, node_list, back_grad, back_count = items
        gradient = grad_table[:, :node_count].at[:, node_list].add(back_grad)
        touched = count_table[:node_count].at[node_list].add(back_count)
        return -jnp.where(touched > 0.5, gradient, 0.0)
    descents = lax.map(assemble, (grad_tables, count_tables, node_lists, back_grads, back_counts))
    halo_descents = jnp.roll(jnp.take_along_axis(descents, node_lists[:, None, :], axis=2), -1, axis=0)

    def second_pass(items):
        values, lower_halo, upper_halo, neighbour_list, corner_list, place, halo_place, descent, halo_descent, flag_row = items
        outer_states = neighbour_states(face_traces(values), lower_halo, upper_halo, far_field, neighbour_list)
        corners = jnp.take(jnp.concatenate([place, halo_place], axis=1), corner_list, axis=1)
        corner_step = jnp.take(jnp.concatenate([descent, halo_descent], axis=1), corner_list, axis=1)
        change = jax.jvp(lambda c: element_residual(values, outer_states, c), (corners,), (corner_step,))[1]
        weight = flag_row.astype(jnp.float32)
        curvature = jnp.sum(weight * change * change)
        bending = smoothing * jnp.sum(weight * lax.optimization_barrier(jnp.sum(corner_step * jnp.einsum('ike,kl->ile', corner_step, laplacian, precision=HIGHEST), axis=(0, 1))))
        return (curvature, bending)
    curvatures, bendings = lax.map(second_pass, (states, lower_halos, upper_halos, neighbour_lists, corner_lists, places, halo_places, descents, halo_descents, flag_rows))
    norm_total = jnp.sum(descents * descents)
    step_size = norm_total / (jnp.sum(curvatures) + jnp.sum(bendings) + strength * norm_total)
    return (partition_minor(residuals), partition_minor(changes), partition_minor(step_size * descents))
```

```python
import functools
import math

import jax
import jax.numpy as jnp
import numpy as np
from jax import lax
from jax.experimental import pallas as pl
from jax.experimental.pallas import tpu as pltpu
from jax.sharding import PartitionSpec as P

SOFT = 0.01
HIGHEST = lax.Precision.HIGHEST
MESH = pl.DeviceIdType.MESH
F32 = jnp.float32
OTHER = 4096
LANES = 128
FACE = 16
POINTS = 64


def lobatto_tables():
    points = np.array([-1.0, -math.sqrt(0.2), math.sqrt(0.2), 1.0])
    weights = np.array([1.0, 5.0, 5.0, 1.0]) / 6.0
    derivative = np.zeros((4, 4))
    for a in range(4):
        for b in range(4):
            if a == b:
                derivative[a, b] = sum((1.0 / (points[a] - points[m]) for m in range(4) if m != a))
            else:
                numerator = 1.0
                denominator = 1.0
                for m in range(4):
                    if m != b:
                        denominator *= points[b] - points[m]
                        if m != a:
                            numerator *= points[a] - points[m]
                derivative[a, b] = numerator / denominator
    return (points, weights, derivative)


def shape_gradients():
    points = lobatto_tables()[0]
    gradients = np.zeros((3, 64, 8))
    for q in range(64):
        position = (q // 16, q // 4 % 4, q % 4)
        for k in range(8):
            corner_bits = (k // 4, k // 2 % 2, k % 2)
            for j in range(3):
                factor = 1.0
                for m in range(3):
                    orient = 1.0 if corner_bits[m] == 1 else -1.0
                    if m == j:
                        factor *= 0.5 * orient
                    else:
                        factor *= 0.5 * (1.0 + orient * points[position[m]])
                gradients[j, q, k] = factor
    return gradients


def edge_laplacian():
    matrix = np.zeros((8, 8))
    for k in range(8):
        matrix[k, k] = 3.0
        for b in range(3):
            matrix[k, k ^ 1 << b] = -1.0
    return matrix


def tables():
    _, weights, derivative = lobatto_tables()
    gradients = shape_gradients()
    grid = np.arange(64).reshape(4, 4, 4)
    face_rows = [np.take(grid, 3 * (f % 2), axis=f // 2).reshape(-1) for f in range(6)]
    select = np.zeros((96, 64))
    select[np.arange(96), np.concatenate(face_rows)] = 1.0
    volume = (weights[:, None, None] * weights[None, :, None] * weights[None, None, :]).reshape(-1)
    face_weights = np.tile((weights[:, None] * weights[None, :]).reshape(-1), 6)
    eye = np.eye(4)
    applied = [
        np.kron(derivative, np.kron(eye, eye)),
        np.kron(eye, np.kron(derivative, eye)),
        np.kron(eye, np.kron(eye, derivative)),
    ]
    assembly = np.concatenate(
        [volume[:, None] * m for m in applied] + [select.T * face_weights[None, :]], axis=1
    )
    first = [gradients[(f // 2 + 1) % 3][face_rows[f]] * (2.0 * (f % 2) - 1.0) for f in range(6)]
    second = [gradients[(f // 2 + 2) % 3][face_rows[f]] for f in range(6)]
    tangents = np.concatenate([gradients.reshape(192, 8)] + first + second, axis=0)
    arrays = (select, assembly, assembly.T, tangents, tangents.T, edge_laplacian())
    return [np.ascontiguousarray(a, dtype=np.float32) for a in arrays]


def mm(a, b):
    return jnp.dot(a, b, precision=HIGHEST, preferred_element_type=F32)


def mm_t(a, b):
    return lax.dot_general(
        a, b, (((1,), (1,)), ((), ())), precision=HIGHEST, preferred_element_type=F32
    )


def cross(a, b):
    return [
        a[1] * b[2] - a[2] * b[1],
        a[2] * b[0] - a[0] * b[2],
        a[0] * b[1] - a[1] * b[0],
    ]


def dot3(a, b):
    return a[0] * b[0] + a[1] * b[1] + a[2] * b[2]


class Gas:
    def __init__(self, values, tangent):
        self.u, self.du = values, tangent
        self.m, self.dm = values[1:4], tangent[1:4]
        self.inv = 1.0 / values[0]
        self.v = [m * self.inv for m in self.m]
        self.p = 0.4 * (values[4] - 0.5 * dot3(self.m, self.v))
        self.h = values[4] + self.p
        self.dv = [(self.dm[i] - self.v[i] * tangent[0]) * self.inv for i in range(3)]
        self.dp = 0.4 * (tangent[4] - 0.5 * (dot3(self.dm, self.v) + dot3(self.m, self.dv)))
        self.dh = tangent[4] + self.dp

    def along(self, n):
        vn = dot3(self.v, n)
        return [dot3(self.m, n)] + [self.m[k] * vn + self.p * n[k] for k in range(3)] + [self.h * vn]

    def along_change(self, n):
        vn, dvn = dot3(self.v, n), dot3(self.dv, n)
        middle = [self.dm[k] * vn + self.m[k] * dvn + self.dp * n[k] for k in range(3)]
        return [dot3(self.dm, n)] + middle + [self.dh * vn + self.h * dvn]

    def against(self, y):
        common = y[1] * self.m[0] + y[2] * self.m[1] + y[3] * self.m[2] + y[4] * self.h
        return [y[0] * self.m[i] + self.v[i] * common + y[1 + i] * self.p for i in range(3)]

    def speed(self, n, square, size):
        a = dot3(self.v, n)
        root = jnp.sqrt(a * a + SOFT * square)
        sound = jnp.sqrt(1.4 * self.p * self.inv)
        inv_root = 1.0 / root
        da = dot3(self.dv, n)
        dsound = 0.7 * (self.dp - self.p * self.du[0] * self.inv) * self.inv / sound
        change = a * da * inv_root + dsound * size
        av, sn = a * inv_root, SOFT * inv_root + sound / size
        return root + sound * size, change, [av * self.v[i] + sn * n[i] for i in range(3)]


def kernel(n, group, *refs):
    (state_ref, tangent_ref, far_ref, place_ref, damp_ref, neigh_ref, nodes_ref, upper_ref, lower_ref,
     sends_ref, flag_ref, select_ref, asm_ref, asm_t_ref, geo_ref, geo_t_ref, lap_ref,
     res_ref, change_ref, update_ref,
     up_out, up_in, down_out, down_in, place_out, place_in,
     gup_out, gup_in, gdown_out, gdown_in, sum_out, sum_in, send_sem, recv_sem) = refs
    me = lax.axis_index("parts")
    right, left = lax.rem(me + 1, n), lax.rem(me + n - 1, n)
    elements = state_ref.shape[2]
    slots = upper_ref.shape[1]
    owned = place_ref.shape[1]
    shared = sends_ref.shape[1]
    own_pad = -(-owned // LANES) * LANES
    halo_pad = -(-shared // LANES) * LANES
    wide = 2 * elements

    stages = []
    low = 1
    while low < n:
        size = min(group, n // low)
        stages.append([low * k for k in range(1, size)])
        low *= size
    masks = [m for stage in stages for m in stage]

    def partner(mask):
        bit = me // mask % 2 if mask & (mask - 1) == 0 else None
        if bit is not None:
            return me + mask * (1 - 2 * bit)
        result = me
        b = 1
        while b <= mask:
            if mask & b:
                result = result + b * (1 - 2 * (me // b % 2))
            b *= 2
        return result

    partners = [partner(m) for m in masks]

    def remote(index, src, dst, device):
        return pltpu.make_async_remote_copy(
            src_ref=src, dst_ref=dst, send_sem=send_sem.at[index], recv_sem=recv_sem.at[index],
            device_id=(device,), device_id_type=MESH,
        )

    barrier = pltpu.get_barrier_semaphore()
    for device in [left, right] + partners:
        pl.semaphore_signal(barrier, inc=1, device_id=(device,), device_id_type=MESH)

    own_rows = lax.broadcasted_iota(jnp.int32, (own_pad, halo_pad), 0)
    sends = sends_ref[...]
    if halo_pad > shared:
        sends = jnp.concatenate([sends, jnp.full((1, halo_pad - shared), -1, jnp.int32)], axis=1)
    sent_nodes = jnp.where(own_rows == sends, 1.0, 0.0).astype(F32)
    places = jnp.zeros((8, own_pad), F32)
    place = place_ref[...]
    if own_pad > owned:
        place = jnp.concatenate([place, jnp.zeros((3, own_pad - owned), F32)], axis=1)
    places = jnp.concatenate([place, jnp.zeros((5, own_pad), F32)], axis=0)
    place_out[...] = mm(places, sent_nodes)

    row = lax.broadcasted_iota(jnp.int32, (wide, wide), 0)
    in_tangent = row >= elements
    local_key = jnp.where(in_tangent, row - elements + OTHER, row)
    slot = jnp.where(in_tangent, row - elements, row)
    halo_key = jnp.where(slot < slots, local_key + elements, -1)

    def one_hot(key, index):
        return jnp.where(key == index, 1.0, 0.0).astype(F32)

    def send_hot(index):
        if slots < elements:
            pad = jnp.full((1, elements - slots), -2, jnp.int32)
            index = jnp.concatenate([index, pad, index + OTHER, pad], axis=1)
        else:
            index = jnp.concatenate([index, index + OTHER], axis=1)
        return one_hot(local_key, index)

    values = [state_ref[v] for v in range(5)]
    tangent = [tangent_ref[v] for v in range(5)]
    both = [jnp.concatenate([values[v], tangent[v]], axis=1) for v in range(5)]
    top = POINTS - FACE
    up_out[...] = mm(
        jnp.concatenate([both[v][top:POINTS] for v in range(5)], axis=0), send_hot(upper_ref[...])
    )
    down_out[...] = mm(
        jnp.concatenate([both[v][0:FACE] for v in range(5)], axis=0), send_hot(lower_ref[...])
    )
    pl.semaphore_wait(barrier, 2 + len(partners))
    place_copy = remote(0, place_out, place_in, left)
    up_copy = remote(1, up_out, up_in, right)
    down_copy = remote(2, down_out, down_in, left)
    place_copy.start()
    up_copy.start()
    down_copy.start()

    weight = flag_ref[...].astype(F32)
    gas = Gas(values, tangent)
    select = select_ref[...]
    trace = [mm(select, both[v]) for v in range(5)]
    neigh = neigh_ref[...]
    neigh = jnp.concatenate([neigh, neigh + OTHER], axis=1)
    far = jnp.where(neigh == elements + slots, 1.0, 0.0).astype(F32)
    outer = []
    for f in range(6):
        opposite = FACE * (f ^ 1)
        stack = jnp.concatenate([trace[v][opposite:opposite + FACE] for v in range(5)], axis=0)
        found = mm(stack, one_hot(local_key, neigh[f:f + 1]))
        outer.append(found)
    nodes = nodes_ref[...]
    nodes = jnp.where(nodes >= owned, nodes + (own_pad - owned), nodes)
    nodes = jnp.concatenate([nodes[k:k + 1] for k in range(8)], axis=1)
    table_rows = lax.broadcasted_iota(jnp.int32, (own_pad + halo_pad, 8 * elements), 0)
    corner_hot = one_hot(table_rows, nodes)

    def corners_of(table):
        found = mm(table, corner_hot)
        return [
            jnp.concatenate(
                [found[i:i + 1, k * elements:(k + 1) * elements] for k in range(8)], axis=0
            )
            for i in range(3)
        ]

    geo = geo_ref[...]

    def edges_of(corners):
        rows = [mm(geo, corners[i]) for i in range(3)]
        volume = [[rows[i][POINTS * j:POINTS * (j + 1)] for i in range(3)] for j in range(3)]
        base = 3 * POINTS
        first = [rows[i][base:base + 6 * FACE] for i in range(3)]
        second = [rows[i][base + 6 * FACE:base + 12 * FACE] for i in range(3)]
        return volume, first, second

    place_copy.wait()
    corners = corners_of(jnp.concatenate([places, place_in[...]], axis=1))
    edge, first, second = edges_of(corners)
    normals = [cross(edge[(j + 1) % 3], edge[(j + 2) % 3]) for j in range(3)]
    face_n = cross(first, second)
    square = dot3(face_n, face_n)
    size = jnp.sqrt(square)

    flux = [gas.along(normals[j]) for j in range(3)]
    flux_change = [gas.along_change(normals[j]) for j in range(3)]
    inner = Gas([t[:, :elements] for t in trace], [t[:, elements:] for t in trace])
    inner_speed, inner_dspeed, inner_grad = inner.speed(face_n, square, size)

    up_copy.wait()
    outer[0] = outer[0] + mm(up_in[...], one_hot(halo_key, neigh[0:1]))
    down_copy.wait()
    outer[1] = outer[1] + mm(down_in[...], one_hot(halo_key, neigh[1:2]))
    side = []
    for v in range(5):
        side.append(
            jnp.concatenate(
                [
                    outer[f][FACE * v:FACE * (v + 1)] + far[f:f + 1] * far_ref[v]
                    for f in range(6)
                ],
                axis=0,
            )
        )
    other = Gas([t[:, :elements] for t in side], [t[:, elements:] for t in side])
    other_speed, other_dspeed, other_grad = other.speed(face_n, square, size)
    gap = inner_speed - other_speed
    root = jnp.sqrt(gap * gap + SOFT * square)
    inv_root = 0.5 / root
    lam = 0.5 * (inner_speed + other_speed) + 0.5 * root
    dlam = 0.5 * (inner_dspeed + other_dspeed) + gap * (inner_dspeed - other_dspeed) * inv_root
    lam_n = [
        0.5 * (inner_grad[i] + other_grad[i])
        + (gap * (inner_grad[i] - other_grad[i]) + SOFT * face_n[i]) * inv_root
        for i in range(3)
    ]
    diff = [other.u[v] - inner.u[v] for v in range(5)]
    ddiff = [other.du[v] - inner.du[v] for v in range(5)]
    inner_along, other_along = inner.along(face_n), other.along(face_n)
    inner_change, other_change = inner.along_change(face_n), other.along_change(face_n)
    asm = asm_ref[...]
    weighted = []
    for v in range(5):
        jump = 0.5 * (other_along[v] - inner_along[v] - lam * diff[v])
        djump = 0.5 * (other_change[v] - inner_change[v] - dlam * diff[v] - lam * ddiff[v])
        primal = jnp.concatenate([flux[0][v], flux[1][v], flux[2][v], jump], axis=0)
        change = jnp.concatenate(
            [flux_change[0][v], flux_change[1][v], flux_change[2][v], djump], axis=0
        )
        result = mm(asm, jnp.concatenate([primal, change], axis=1))
        res_ref[v] = result[:, :elements]
        change_ref[v] = result[:, elements:]
        weighted.append(result[:, :elements] * weight)

    asm_t = asm_t_ref[...]
    back = [mm(asm_t, weighted[v]) for v in range(5)]
    grads = [gas.against([b[POINTS * j:POINTS * (j + 1)] for b in back]) for j in range(3)]
    face_back = [b[3 * POINTS:] for b in back]
    across = sum(face_back[v] * diff[v] for v in range(5))
    inner_against, other_against = inner.against(face_back), other.against(face_back)
    face_grad = [
        0.5 * (other_against[i] - inner_against[i] - across * lam_n[i]) for i in range(3)
    ]
    edge_grad = []
    for j in range(3):
        one = cross(edge[(j + 1) % 3], grads[(j + 2) % 3])
        two = cross(grads[(j + 1) % 3], edge[(j + 2) % 3])
        edge_grad.append([one[i] + two[i] for i in range(3)])
    first_grad, second_grad = cross(second, face_grad), cross(face_grad, first)
    smoothing = damp_ref[1]
    lap = lap_ref[...]
    geo_t = geo_t_ref[...]
    rows = []
    for i in range(3):
        stack = jnp.concatenate(
            [edge_grad[0][i], edge_grad[1][i], edge_grad[2][i], first_grad[i], second_grad[i]], axis=0
        )
        corner_grad = mm(geo_t, stack) + smoothing * weight * mm(lap, corners[i])
        rows.append(jnp.concatenate([corner_grad[k:k + 1] for k in range(8)], axis=1))
    rows.append(jnp.concatenate([weight] * 8, axis=1))
    rows.append(jnp.zeros((4, 8 * elements), F32))
    table = mm_t(jnp.concatenate(rows, axis=0), corner_hot)
    own_part, halo_part = table[:, :own_pad], table[:, own_pad:]

    gup_out[...] = halo_part
    gup_copy = remote(3, gup_out, gup_in, right)
    gup_copy.start()
    gdown_out[...] = mm(own_part, sent_nodes)
    gdown_copy = remote(4, gdown_out, gdown_in, left)
    gdown_copy.start()

    def descent_of(total):
        line = lax.broadcasted_iota(jnp.int32, total.shape, 0)
        touched = jnp.where(total[3:4] > 0.5, 1.0, 0.0)
        return -jnp.where(line < 3, total * touched, 0.0)

    gup_copy.wait()
    descent = descent_of(own_part + mm_t(gup_in[...], sent_nodes))
    gdown_copy.wait()
    halo_descent = descent_of(halo_part + gdown_in[...])

    steps = corners_of(jnp.concatenate([descent, halo_descent], axis=1))
    dedge, dfirst, dsecond = edges_of(steps)
    dflux = []
    for j in range(3):
        a, b = (j + 1) % 3, (j + 2) % 3
        one, two = cross(dedge[a], edge[b]), cross(edge[a], dedge[b])
        dflux.append(gas.along([one[i] + two[i] for i in range(3)]))
    one, two = cross(dfirst, second), cross(first, dsecond)
    dface = [one[i] + two[i] for i in range(3)]
    inner_dalong, other_dalong = inner.along(dface), other.along(dface)
    dlam_n = dot3(lam_n, dface)
    total = jnp.zeros((POINTS, elements), F32)
    for v in range(5):
        jump = 0.5 * (other_dalong[v] - inner_dalong[v] - dlam_n * diff[v])
        moved = mm(asm, jnp.concatenate([dflux[0][v], dflux[1][v], dflux[2][v], jump], axis=0))
        total = total + moved * moved
    curvature = jnp.sum(total, axis=0, keepdims=True) * weight
    bent = sum(steps[i] * mm(lap, steps[i]) for i in range(3))
    bending = smoothing * jnp.sum(bent, axis=0, keepdims=True) * weight
    norm = jnp.sum(descent * descent, axis=0, keepdims=True)
    both_sums = jnp.sum(curvature + bending, axis=1, keepdims=True)
    norm_sum = jnp.sum(norm, axis=1, keepdims=True)
    line = lax.broadcasted_iota(jnp.int32, (8, LANES), 0)
    sums = jnp.where(line == 0, norm_sum, jnp.where(line == 1, both_sums, 0.0))

    index = 0
    for s, stage in enumerate(stages):
        sum_out[s] = sums
        copies = []
        for _ in stage:
            copies.append(remote(5 + index, sum_out.at[s], sum_in.at[index], partners[index]))
            copies[-1].start()
            index += 1
        for i, copy in enumerate(copies):
            copy.wait_recv()
        for i in range(len(stage)):
            sums = sums + sum_in[index - len(stage) + i]
        for copy in copies:
            copy.wait_send()
    norm_total, rest = sums[0:1, 0:1], sums[1:2, 0:1]
    step_size = norm_total / (rest + damp_ref[0] * norm_total)
    update_ref[...] = (descent * step_size)[0:3, :owned]


def body(n, group, flow_state, state_tangent, far_field, coordinates, damping, face_neighbour,
         element_nodes, upper_sends, lower_sends, node_sends, shock_flags):
    own_pad = -(-coordinates.shape[1] // LANES) * LANES
    halo_pad = -(-node_sends.shape[0] // LANES) * LANES
    wide = 2 * flow_state.shape[2]
    count, stages, low = 0, 0, 1
    while low < n:
        size = min(group, n // low)
        count, stages, low = count + size - 1, stages + 1, low * size
    vmem = pl.BlockSpec(memory_space=pltpu.VMEM)
    smem = pl.BlockSpec(memory_space=pltpu.SMEM)
    constants = [jnp.asarray(t) for t in tables()]
    halo = pltpu.VMEM((5 * FACE, wide), F32)
    place = pltpu.VMEM((8, halo_pad), F32)
    operands = [
        flow_state, state_tangent, far_field, coordinates, damping, face_neighbour, element_nodes,
        upper_sends.reshape(1, -1), lower_sends.reshape(1, -1), node_sends.reshape(1, -1),
        shock_flags.reshape(1, -1),
    ] + constants
    specs = [vmem] * len(operands)
    specs[2] = specs[4] = smem
    return pl.pallas_call(
        functools.partial(kernel, n, group),
        out_shape=(
            jax.ShapeDtypeStruct(flow_state.shape, F32),
            jax.ShapeDtypeStruct(flow_state.shape, F32),
            jax.ShapeDtypeStruct(coordinates.shape, F32),
        ),
        in_specs=specs,
        out_specs=(vmem, vmem, vmem),
        scratch_shapes=[halo] * 4 + [place] * 6 + [
            pltpu.VMEM((stages, 8, LANES), F32),
            pltpu.VMEM((count, 8, LANES), F32),
            pltpu.SemaphoreType.DMA((5 + count,)),
            pltpu.SemaphoreType.DMA((5 + count,)),
        ],
        compiler_params=pltpu.CompilerParams(
            collective_id=0, has_side_effects=True, vmem_limit_bytes=48 * 1024 * 1024
        ),
    )(*operands)


def solution(mesh):
    n = mesh.shape["parts"]
    in_specs = (
        P(None, None, "parts"),
        P(None, None, "parts"),
        P(),
        P(None, "parts"),
        P(),
        P(None, "parts"),
        P(None, "parts"),
        P("parts"),
        P("parts"),
        P("parts"),
        P("parts"),
    )
    out_specs = (P(None, None, "parts"), P(None, None, "parts"), P(None, "parts"))
    return jax.shard_map(
        functools.partial(body, n, 8), mesh=mesh, in_specs=in_specs, out_specs=out_specs,
        check_vma=False,
    )
```

```python
import functools
import math

import jax
import jax.numpy as jnp
import ml_dtypes
import numpy as np
from jax import lax
from jax.experimental import pallas as pl
from jax.experimental.pallas import tpu as pltpu
from jax.sharding import PartitionSpec as P

SOFT = 0.01
MESH = pl.DeviceIdType.MESH
F32 = jnp.float32
BF16 = jnp.bfloat16
OTHER = 4096
INPUTS = 16
VMEM_LIMIT = 60 * 1024 * 1024
LOAD_ORDER = (9, 3, 7, 8, 0, 1, 11, 5, 6, 14, 2, 4, 10, 12, 13, 15)
LANES = 128
FACE = 16
POINTS = 64


def lobatto_tables():
    points = np.array([-1.0, -math.sqrt(0.2), math.sqrt(0.2), 1.0])
    weights = np.array([1.0, 5.0, 5.0, 1.0]) / 6.0
    derivative = np.zeros((4, 4))
    for a in range(4):
        for b in range(4):
            if a == b:
                derivative[a, b] = sum((1.0 / (points[a] - points[m]) for m in range(4) if m != a))
            else:
                numerator = 1.0
                denominator = 1.0
                for m in range(4):
                    if m != b:
                        denominator *= points[b] - points[m]
                        if m != a:
                            numerator *= points[a] - points[m]
                derivative[a, b] = numerator / denominator
    return (points, weights, derivative)


def shape_gradients():
    points = lobatto_tables()[0]
    gradients = np.zeros((3, 64, 8))
    for q in range(64):
        position = (q // 16, q // 4 % 4, q % 4)
        for k in range(8):
            corner_bits = (k // 4, k // 2 % 2, k % 2)
            for j in range(3):
                factor = 1.0
                for m in range(3):
                    orient = 1.0 if corner_bits[m] == 1 else -1.0
                    if m == j:
                        factor *= 0.5 * orient
                    else:
                        factor *= 0.5 * (1.0 + orient * points[position[m]])
                gradients[j, q, k] = factor
    return gradients


def edge_laplacian():
    matrix = np.zeros((8, 8))
    for k in range(8):
        matrix[k, k] = 3.0
        for b in range(3):
            matrix[k, k ^ 1 << b] = -1.0
    return matrix


def tables():
    _, weights, derivative = lobatto_tables()
    gradients = shape_gradients()
    grid = np.arange(64).reshape(4, 4, 4)
    face_rows = [np.take(grid, 3 * (f % 2), axis=f // 2).reshape(-1) for f in range(6)]
    select = np.zeros((96, 64))
    select[np.arange(96), np.concatenate(face_rows)] = 1.0
    volume = (weights[:, None, None] * weights[None, :, None] * weights[None, None, :]).reshape(-1)
    face_weights = np.tile((weights[:, None] * weights[None, :]).reshape(-1), 6)
    eye = np.eye(4)
    applied = [
        np.kron(derivative, np.kron(eye, eye)),
        np.kron(eye, np.kron(derivative, eye)),
        np.kron(eye, np.kron(eye, derivative)),
    ]
    assembly = np.concatenate(
        [volume[:, None] * m for m in applied] + [select.T * face_weights[None, :]], axis=1
    )
    first = [gradients[(f // 2 + 1) % 3][face_rows[f]] * (2.0 * (f % 2) - 1.0) for f in range(6)]
    second = [gradients[(f // 2 + 2) % 3][face_rows[f]] for f in range(6)]
    tangents = np.concatenate([gradients.reshape(192, 8)] + first + second, axis=0)
    hi, mid, lo = split_table(np.concatenate([tangents, edge_laplacian()], axis=0))
    arrays = (
        np.concatenate([select] * 3, axis=1),
        two_parts(assembly),
        two_parts(assembly.T),
        np.concatenate([hi, hi, hi, mid, mid, lo], axis=1),
        two_parts(tangents.T),
    )
    return [np.ascontiguousarray(a, dtype=np.float32) for a in arrays]


def split_table(a):
    parts, rest = [], a
    for _ in range(3):
        part = rest.astype(ml_dtypes.bfloat16).astype(np.float64)
        parts.append(part)
        rest = rest - part
    return parts


def two_parts(a):
    hi, mid, _ = split_table(a)
    return np.concatenate([hi, mid, hi], axis=1)


def split(x, count):
    parts = []
    for _ in range(count - 1):
        part = x.astype(BF16).astype(F32)
        parts.append(part)
        x = x - part
    return parts + [x]


def rows_of(parts):
    return jnp.concatenate(parts, axis=0).astype(BF16)


def apply_table(table, data):
    hi, lo = split(data, 2)
    return jnp.dot(table, rows_of([hi, hi, lo]), preferred_element_type=F32)


def pick(data, hot):
    count = data.shape[0]
    out = jnp.dot(rows_of(split(data, 3)), hot, preferred_element_type=F32)
    return out[:count] + out[count:2 * count] + out[2 * count:]


def pick_t(data, hot):
    count = data.shape[0]
    out = lax.dot_general(
        rows_of(split(data, 3)), hot, (((1,), (1,)), ((), ())), preferred_element_type=F32
    )
    return out[:count] + out[count:2 * count] + out[2 * count:]


def cross(a, b):
    return [
        a[1] * b[2] - a[2] * b[1],
        a[2] * b[0] - a[0] * b[2],
        a[0] * b[1] - a[1] * b[0],
    ]


def dot3(a, b):
    return a[0] * b[0] + a[1] * b[1] + a[2] * b[2]


class Gas:
    def __init__(self, values, tangent):
        self.u, self.du = values, tangent
        self.m, self.dm = values[1:4], tangent[1:4]
        self.inv = 1.0 / values[0]
        self.v = [m * self.inv for m in self.m]
        self.p = 0.4 * (values[4] - 0.5 * dot3(self.m, self.v))
        self.h = values[4] + self.p
        self.dv = [(self.dm[i] - self.v[i] * tangent[0]) * self.inv for i in range(3)]
        self.dp = 0.4 * (tangent[4] - 0.5 * (dot3(self.dm, self.v) + dot3(self.m, self.dv)))
        self.dh = tangent[4] + self.dp

    def along(self, n):
        vn = dot3(self.v, n)
        return [dot3(self.m, n)] + [self.m[k] * vn + self.p * n[k] for k in range(3)] + [self.h * vn]

    def along_change(self, n):
        vn, dvn = dot3(self.v, n), dot3(self.dv, n)
        middle = [self.dm[k] * vn + self.m[k] * dvn + self.dp * n[k] for k in range(3)]
        return [dot3(self.dm, n)] + middle + [self.dh * vn + self.h * dvn]

    def against(self, y):
        common = y[1] * self.m[0] + y[2] * self.m[1] + y[3] * self.m[2] + y[4] * self.h
        return [y[0] * self.m[i] + self.v[i] * common + y[1 + i] * self.p for i in range(3)]

    def speed(self, n, square, size):
        a = dot3(self.v, n)
        root = jnp.sqrt(a * a + SOFT * square)
        sound = jnp.sqrt(1.4 * self.p * self.inv)
        inv_root = 1.0 / root
        da = dot3(self.dv, n)
        dsound = 0.7 * (self.dp - self.p * self.du[0] * self.inv) * self.inv / sound
        change = a * da * inv_root + dsound * size
        av, sn = a * inv_root, SOFT * inv_root + sound / size
        return root + sound * size, change, [av * self.v[i] + sn * n[i] for i in range(3)]


def kernel(n, group, *refs):
    sources, refs = refs[:INPUTS], refs[INPUTS:]
    results, refs = refs[:3], refs[3:]
    held, refs = refs[:INPUTS], refs[INPUTS:]
    (res_ref, change_ref, update_ref), refs = refs[:3], refs[3:]
    (state_ref, tangent_ref, far_ref, place_ref, damp_ref, neigh_ref, nodes_ref, upper_ref, lower_ref,
     sends_ref, flag_ref, select_ref, asm_ref, asm_t_ref, geo_ref, geo_t_ref) = held
    (up_out, up_in, down_out, down_in, place_out, place_in,
     gup_out, gup_in, gdown_out, gdown_in, sum_out, sum_in, send_sem, recv_sem, load_sem) = refs
    loads = [
        pltpu.make_async_copy(sources[i], held[i], load_sem.at[i]) for i in range(INPUTS)
    ]
    stores = [
        pltpu.make_async_copy(source, results[i], load_sem.at[INPUTS + i])
        for i, source in enumerate((res_ref, change_ref, update_ref))
    ]
    for i in LOAD_ORDER:
        loads[i].start()
    me = lax.axis_index("parts")
    right, left = lax.rem(me + 1, n), lax.rem(me + n - 1, n)
    elements = state_ref.shape[2]
    slots = upper_ref.shape[1]
    owned = place_ref.shape[1]
    shared = sends_ref.shape[1]
    own_pad = -(-owned // LANES) * LANES
    halo_pad = -(-shared // LANES) * LANES
    wide = 2 * elements

    stages = []
    low = 1
    while low < n:
        size = min(group, n // low)
        stages.append([low * k for k in range(1, size)])
        low *= size
    masks = [m for stage in stages for m in stage]

    def partner(mask):
        bit = me // mask % 2 if mask & (mask - 1) == 0 else None
        if bit is not None:
            return me + mask * (1 - 2 * bit)
        result = me
        b = 1
        while b <= mask:
            if mask & b:
                result = result + b * (1 - 2 * (me // b % 2))
            b *= 2
        return result

    partners = [partner(m) for m in masks]

    def remote(index, src, dst, device):
        return pltpu.make_async_remote_copy(
            src_ref=src, dst_ref=dst, send_sem=send_sem.at[index], recv_sem=recv_sem.at[index],
            device_id=(device,), device_id_type=MESH,
        )

    barrier = pltpu.get_barrier_semaphore()
    for device in [left, right] + partners:
        pl.semaphore_signal(barrier, inc=1, device_id=(device,), device_id_type=MESH)

    for i in LOAD_ORDER[:6]:
        loads[i].wait()
    own_rows = lax.broadcasted_iota(jnp.int32, (own_pad, halo_pad), 0)
    sends = sends_ref[...]
    if halo_pad > shared:
        sends = jnp.concatenate([sends, jnp.full((1, halo_pad - shared), -1, jnp.int32)], axis=1)
    sent_nodes = jnp.where(own_rows == sends, 1.0, 0.0).astype(BF16)
    places = jnp.zeros((8, own_pad), F32)
    place = place_ref[...]
    if own_pad > owned:
        place = jnp.concatenate([place, jnp.zeros((3, own_pad - owned), F32)], axis=1)
    places = jnp.concatenate([place, jnp.zeros((5, own_pad), F32)], axis=0)
    place_out[...] = pick(places, sent_nodes)

    row = lax.broadcasted_iota(jnp.int32, (wide, wide), 0)
    in_tangent = row >= elements
    local_key = jnp.where(in_tangent, row - elements + OTHER, row)
    slot = jnp.where(in_tangent, row - elements, row)
    halo_key = jnp.where(slot < slots, local_key + elements, -1)

    def one_hot(key, index):
        return jnp.where(key == index, 1.0, 0.0).astype(BF16)

    def send_hot(index):
        if slots < elements:
            pad = jnp.full((1, elements - slots), -2, jnp.int32)
            index = jnp.concatenate([index, pad, index + OTHER, pad], axis=1)
        else:
            index = jnp.concatenate([index, index + OTHER], axis=1)
        return one_hot(local_key, index)

    values = [state_ref[v] for v in range(5)]
    tangent = [tangent_ref[v] for v in range(5)]
    both = [jnp.concatenate([values[v], tangent[v]], axis=1) for v in range(5)]
    top = POINTS - FACE
    up_out[...] = pick(
        jnp.concatenate([both[v][top:POINTS] for v in range(5)], axis=0), send_hot(upper_ref[...])
    )
    down_out[...] = pick(
        jnp.concatenate([both[v][0:FACE] for v in range(5)], axis=0), send_hot(lower_ref[...])
    )
    pl.semaphore_wait(barrier, 2 + len(partners))
    place_copy = remote(0, place_out, place_in, left)
    up_copy = remote(1, up_out, up_in, right)
    down_copy = remote(2, down_out, down_in, left)
    place_copy.start()
    up_copy.start()
    down_copy.start()

    for i in LOAD_ORDER[6:]:
        loads[i].wait()
    weight = flag_ref[...].astype(F32)
    far_field = far_ref[...]
    damping = damp_ref[...]
    gas = Gas(values, tangent)
    select = select_ref[...].astype(BF16)
    traces = jnp.dot(
        select, rows_of(split(jnp.concatenate(both, axis=1), 3)), preferred_element_type=F32
    )
    trace = [traces[:, v * wide:(v + 1) * wide] for v in range(5)]
    neigh = neigh_ref[...]
    neigh = jnp.concatenate([neigh, neigh + OTHER], axis=1)
    far = jnp.where(neigh == elements + slots, 1.0, 0.0).astype(F32)
    outer = []
    for f in range(6):
        opposite = FACE * (f ^ 1)
        stack = jnp.concatenate([trace[v][opposite:opposite + FACE] for v in range(5)], axis=0)
        found = pick(stack, one_hot(local_key, neigh[f:f + 1]))
        outer.append(found)
    nodes = nodes_ref[...]
    nodes = jnp.where(nodes >= owned, nodes + (own_pad - owned), nodes)
    nodes = jnp.concatenate([nodes[k:k + 1] for k in range(8)], axis=1)
    table_rows = lax.broadcasted_iota(jnp.int32, (own_pad + halo_pad, 8 * elements), 0)
    corner_hot = one_hot(table_rows, nodes)

    def corners_of(table):
        found = pick(table, corner_hot)
        return [
            jnp.concatenate(
                [found[i:i + 1, k * elements:(k + 1) * elements] for k in range(8)], axis=0
            )
            for i in range(3)
        ]

    geo = geo_ref[...].astype(BF16)

    def edges_of(corners):
        hi, mid, lo = split(jnp.concatenate(corners, axis=1), 3)
        out = jnp.dot(geo, rows_of([hi, mid, lo, hi, mid, hi]), preferred_element_type=F32)
        rows = [out[:, i * elements:(i + 1) * elements] for i in range(3)]
        volume = [[rows[i][POINTS * j:POINTS * (j + 1)] for i in range(3)] for j in range(3)]
        base = 3 * POINTS
        first = [rows[i][base:base + 6 * FACE] for i in range(3)]
        second = [rows[i][base + 6 * FACE:base + 12 * FACE] for i in range(3)]
        lap = [rows[i][base + 12 * FACE:] for i in range(3)]
        return volume, first, second, lap

    place_copy.wait()
    corners = corners_of(jnp.concatenate([places, place_in[...]], axis=1))
    edge, first, second, lap = edges_of(corners)
    normals = [cross(edge[(j + 1) % 3], edge[(j + 2) % 3]) for j in range(3)]
    face_n = cross(first, second)
    square = dot3(face_n, face_n)
    size = jnp.sqrt(square)

    flux = [gas.along(normals[j]) for j in range(3)]
    flux_change = [gas.along_change(normals[j]) for j in range(3)]
    inner = Gas([t[:, :elements] for t in trace], [t[:, elements:] for t in trace])
    inner_speed, inner_dspeed, inner_grad = inner.speed(face_n, square, size)

    up_copy.wait()
    outer[0] = outer[0] + pick(up_in[...], one_hot(halo_key, neigh[0:1]))
    down_copy.wait()
    outer[1] = outer[1] + pick(down_in[...], one_hot(halo_key, neigh[1:2]))
    side = []
    for v in range(5):
        side.append(
            jnp.concatenate(
                [
                    outer[f][FACE * v:FACE * (v + 1)] + far[f:f + 1] * far_field[:, v:v + 1]
                    for f in range(6)
                ],
                axis=0,
            )
        )
    other = Gas([t[:, :elements] for t in side], [t[:, elements:] for t in side])
    other_speed, other_dspeed, other_grad = other.speed(face_n, square, size)
    gap = inner_speed - other_speed
    root = jnp.sqrt(gap * gap + SOFT * square)
    inv_root = 0.5 / root
    lam = 0.5 * (inner_speed + other_speed) + 0.5 * root
    dlam = 0.5 * (inner_dspeed + other_dspeed) + gap * (inner_dspeed - other_dspeed) * inv_root
    lam_n = [
        0.5 * (inner_grad[i] + other_grad[i])
        + (gap * (inner_grad[i] - other_grad[i]) + SOFT * face_n[i]) * inv_root
        for i in range(3)
    ]
    diff = [other.u[v] - inner.u[v] for v in range(5)]
    ddiff = [other.du[v] - inner.du[v] for v in range(5)]
    inner_along, other_along = inner.along(face_n), other.along(face_n)
    inner_change, other_change = inner.along_change(face_n), other.along_change(face_n)
    asm = asm_ref[...].astype(BF16)
    columns = []
    for v in range(5):
        jump = 0.5 * (other_along[v] - inner_along[v] - lam * diff[v])
        djump = 0.5 * (other_change[v] - inner_change[v] - dlam * diff[v] - lam * ddiff[v])
        primal = jnp.concatenate([flux[0][v], flux[1][v], flux[2][v], jump], axis=0)
        change = jnp.concatenate(
            [flux_change[0][v], flux_change[1][v], flux_change[2][v], djump], axis=0
        )
        columns.append(jnp.concatenate([primal, change], axis=1))
    result = apply_table(asm, jnp.concatenate(columns, axis=1))
    weighted = []
    for v in range(5):
        residual = result[:, v * wide:v * wide + elements]
        res_ref[v] = residual
        change_ref[v] = result[:, v * wide + elements:(v + 1) * wide]
        weighted.append(residual * weight)

    stores[0].start()
    stores[1].start()

    asm_t = asm_t_ref[...].astype(BF16)
    back = [apply_table(asm_t, weighted[v]) for v in range(5)]
    grads = [gas.against([b[POINTS * j:POINTS * (j + 1)] for b in back]) for j in range(3)]
    face_back = [b[3 * POINTS:] for b in back]
    across = sum(face_back[v] * diff[v] for v in range(5))
    inner_against, other_against = inner.against(face_back), other.against(face_back)
    face_grad = [
        0.5 * (other_against[i] - inner_against[i] - across * lam_n[i]) for i in range(3)
    ]
    edge_grad = []
    for j in range(3):
        one = cross(edge[(j + 1) % 3], grads[(j + 2) % 3])
        two = cross(grads[(j + 1) % 3], edge[(j + 2) % 3])
        edge_grad.append([one[i] + two[i] for i in range(3)])
    first_grad, second_grad = cross(second, face_grad), cross(face_grad, first)
    smoothing = damping[:, 1:2]
    geo_t = geo_t_ref[...].astype(BF16)
    stack = [
        jnp.concatenate(
            [edge_grad[0][i], edge_grad[1][i], edge_grad[2][i], first_grad[i], second_grad[i]], axis=0
        )
        for i in range(3)
    ]
    pulled = apply_table(geo_t, jnp.concatenate(stack, axis=1))
    rows = []
    for i in range(3):
        corner_grad = pulled[:, i * elements:(i + 1) * elements] + smoothing * weight * lap[i]
        rows.append(jnp.concatenate([corner_grad[k:k + 1] for k in range(8)], axis=1))
    rows.append(jnp.concatenate([weight] * 8, axis=1))
    rows.append(jnp.zeros((4, 8 * elements), F32))
    table = pick_t(jnp.concatenate(rows, axis=0), corner_hot)
    own_part, halo_part = table[:, :own_pad], table[:, own_pad:]

    gup_out[...] = halo_part
    gup_copy = remote(3, gup_out, gup_in, right)
    gup_copy.start()
    gdown_out[...] = pick(own_part, sent_nodes)
    gdown_copy = remote(4, gdown_out, gdown_in, left)
    gdown_copy.start()

    def descent_of(total):
        line = lax.broadcasted_iota(jnp.int32, total.shape, 0)
        touched = jnp.where(total[3:4] > 0.5, 1.0, 0.0)
        return -jnp.where(line < 3, total * touched, 0.0)

    gup_copy.wait()
    descent = descent_of(own_part + pick_t(gup_in[...], sent_nodes))
    gdown_copy.wait()
    halo_descent = descent_of(halo_part + gdown_in[...])

    steps = corners_of(jnp.concatenate([descent, halo_descent], axis=1))
    dedge, dfirst, dsecond, dlap = edges_of(steps)
    dflux = []
    for j in range(3):
        a, b = (j + 1) % 3, (j + 2) % 3
        one, two = cross(dedge[a], edge[b]), cross(edge[a], dedge[b])
        dflux.append(gas.along([one[i] + two[i] for i in range(3)]))
    one, two = cross(dfirst, second), cross(first, dsecond)
    dface = [one[i] + two[i] for i in range(3)]
    inner_dalong, other_dalong = inner.along(dface), other.along(dface)
    dlam_n = dot3(lam_n, dface)
    columns = []
    for v in range(5):
        jump = 0.5 * (other_dalong[v] - inner_dalong[v] - dlam_n * diff[v])
        columns.append(jnp.concatenate([dflux[0][v], dflux[1][v], dflux[2][v], jump], axis=0))
    moved = apply_table(asm, jnp.concatenate(columns, axis=1))
    squares = jnp.sum(moved * moved, axis=0, keepdims=True)
    squares = sum(squares[:, v * elements:(v + 1) * elements] for v in range(5))
    curvature = squares * weight
    bent = sum(steps[i] * dlap[i] for i in range(3))
    bending = smoothing * jnp.sum(bent, axis=0, keepdims=True) * weight
    norm = jnp.sum(descent * descent, axis=0, keepdims=True)
    both_sums = jnp.sum(curvature + bending, axis=1, keepdims=True)
    norm_sum = jnp.sum(norm, axis=1, keepdims=True)
    line = lax.broadcasted_iota(jnp.int32, (8, LANES), 0)
    sums = jnp.where(line == 0, norm_sum, jnp.where(line == 1, both_sums, 0.0))

    index = 0
    for s, stage in enumerate(stages):
        sum_out[s] = sums
        copies = []
        for _ in stage:
            copies.append(remote(5 + index, sum_out.at[s], sum_in.at[index], partners[index]))
            copies[-1].start()
            index += 1
        for i, copy in enumerate(copies):
            copy.wait_recv()
        for i in range(len(stage)):
            sums = sums + sum_in[index - len(stage) + i]
        for copy in copies:
            copy.wait_send()
    norm_total, rest = sums[0:1, 0:1], sums[1:2, 0:1]
    step_size = norm_total / (rest + damping[:, 0:1] * norm_total)
    update_ref[...] = (descent * step_size)[0:3, :owned]
    stores[2].start()
    for store in stores:
        store.wait()


def write_out(*refs):
    copies = [pltpu.make_async_copy(refs[i], refs[3 + i], refs[6].at[i]) for i in range(3)]
    for copy in copies:
        copy.start()
    for copy in copies:
        copy.wait()


def body(n, group, flow_state, state_tangent, far_field, coordinates, damping, face_neighbour,
         element_nodes, upper_sends, lower_sends, node_sends, shock_flags):
    own_pad = -(-coordinates.shape[1] // LANES) * LANES
    halo_pad = -(-node_sends.shape[0] // LANES) * LANES
    wide = 2 * flow_state.shape[2]
    count, stages, low = 0, 0, 1
    while low < n:
        size = min(group, n // low)
        count, stages, low = count + size - 1, stages + 1, low * size
    hbm = pl.BlockSpec(memory_space=pltpu.HBM)
    constants = [jnp.asarray(t) for t in tables()]
    halo = pltpu.VMEM((5 * FACE, wide), F32)
    place = pltpu.VMEM((8, halo_pad), F32)
    operands = [
        flow_state, state_tangent, far_field.reshape(1, -1), coordinates, damping.reshape(1, -1),
        face_neighbour, element_nodes,
        upper_sends.reshape(1, -1), lower_sends.reshape(1, -1), node_sends.reshape(1, -1),
        shock_flags.reshape(1, -1),
    ] + constants
    shapes = (
        jax.ShapeDtypeStruct(flow_state.shape, F32),
        jax.ShapeDtypeStruct(flow_state.shape, F32),
        jax.ShapeDtypeStruct(coordinates.shape, F32),
    )
    results = pl.pallas_call(
        functools.partial(kernel, n, group),
        out_shape=shapes,
        in_specs=[hbm] * len(operands),
        out_specs=(hbm, hbm, hbm),
        scratch_shapes=[pltpu.VMEM(o.shape, o.dtype) for o in operands + list(shapes)] + [halo] * 4 + [place] * 6 + [
            pltpu.VMEM((stages, 8, LANES), F32),
            pltpu.VMEM((count, 8, LANES), F32),
            pltpu.SemaphoreType.DMA((5 + count,)),
            pltpu.SemaphoreType.DMA((5 + count,)),
            pltpu.SemaphoreType.DMA((INPUTS + 3,)),
        ],
        compiler_params=pltpu.CompilerParams(
            collective_id=0, has_side_effects=True, vmem_limit_bytes=VMEM_LIMIT
        ),
    )(*operands)
    return pl.pallas_call(
        write_out,
        out_shape=shapes,
        in_specs=[hbm] * 3,
        out_specs=[hbm] * 3,
        scratch_shapes=[pltpu.SemaphoreType.DMA((3,))],
        compiler_params=pltpu.CompilerParams(vmem_limit_bytes=VMEM_LIMIT),
    )(*results)


def solution(mesh):
    n = mesh.shape["parts"]
    in_specs = (
        P(None, None, "parts"),
        P(None, None, "parts"),
        P(),
        P(None, "parts"),
        P(),
        P(None, "parts"),
        P(None, "parts"),
        P("parts"),
        P("parts"),
        P("parts"),
        P("parts"),
    )
    out_specs = (P(None, None, "parts"), P(None, None, "parts"), P(None, "parts"))
    return jax.shard_map(
        functools.partial(body, n, 8), mesh=mesh, in_specs=in_specs, out_specs=out_specs,
        check_vma=False,
    )
```

```python
import functools
import math

import jax
import jax.numpy as jnp
import ml_dtypes
import numpy as np
from jax import lax
from jax.experimental import pallas as pl
from jax.experimental.pallas import tpu as pltpu
from jax.sharding import PartitionSpec as P

SOFT = 0.01
MESH = pl.DeviceIdType.MESH
F32 = jnp.float32
BF16 = jnp.bfloat16
OTHER = 4096
INPUTS = 16
VMEM_LIMIT = 60 * 1024 * 1024
LOAD_ORDER = (9, 3, 7, 8, 0, 1, 11, 5, 6, 14, 2, 4, 10, 12, 13, 15)
LANES = 128
FACE = 16
POINTS = 64


def lobatto_tables():
    points = np.array([-1.0, -math.sqrt(0.2), math.sqrt(0.2), 1.0])
    weights = np.array([1.0, 5.0, 5.0, 1.0]) / 6.0
    derivative = np.zeros((4, 4))
    for a in range(4):
        for b in range(4):
            if a == b:
                derivative[a, b] = sum((1.0 / (points[a] - points[m]) for m in range(4) if m != a))
            else:
                numerator = 1.0
                denominator = 1.0
                for m in range(4):
                    if m != b:
                        denominator *= points[b] - points[m]
                        if m != a:
                            numerator *= points[a] - points[m]
                derivative[a, b] = numerator / denominator
    return (points, weights, derivative)


def shape_gradients():
    points = lobatto_tables()[0]
    gradients = np.zeros((3, 64, 8))
    for q in range(64):
        position = (q // 16, q // 4 % 4, q % 4)
        for k in range(8):
            corner_bits = (k // 4, k // 2 % 2, k % 2)
            for j in range(3):
                factor = 1.0
                for m in range(3):
                    orient = 1.0 if corner_bits[m] == 1 else -1.0
                    if m == j:
                        factor *= 0.5 * orient
                    else:
                        factor *= 0.5 * (1.0 + orient * points[position[m]])
                gradients[j, q, k] = factor
    return gradients


def edge_laplacian():
    matrix = np.zeros((8, 8))
    for k in range(8):
        matrix[k, k] = 3.0
        for b in range(3):
            matrix[k, k ^ 1 << b] = -1.0
    return matrix


def tables():
    _, weights, derivative = lobatto_tables()
    gradients = shape_gradients()
    grid = np.arange(64).reshape(4, 4, 4)
    face_rows = [np.take(grid, 3 * (f % 2), axis=f // 2).reshape(-1) for f in range(6)]
    select = np.zeros((96, 64))
    select[np.arange(96), np.concatenate(face_rows)] = 1.0
    volume = (weights[:, None, None] * weights[None, :, None] * weights[None, None, :]).reshape(-1)
    face_weights = np.tile((weights[:, None] * weights[None, :]).reshape(-1), 6)
    eye = np.eye(4)
    applied = [
        np.kron(derivative, np.kron(eye, eye)),
        np.kron(eye, np.kron(derivative, eye)),
        np.kron(eye, np.kron(eye, derivative)),
    ]
    assembly = np.concatenate(
        [volume[:, None] * m for m in applied] + [select.T * face_weights[None, :]], axis=1
    )
    first = [gradients[(f // 2 + 1) % 3][face_rows[f]] * (2.0 * (f % 2) - 1.0) for f in range(6)]
    second = [gradients[(f // 2 + 2) % 3][face_rows[f]] for f in range(6)]
    tangents = np.concatenate([gradients.reshape(192, 8)] + first + second, axis=0)
    hi, mid, lo = split_table(np.concatenate([tangents, edge_laplacian()], axis=0))
    arrays = (
        np.concatenate([select] * 3, axis=1),
        two_parts(assembly),
        two_parts(assembly.T),
        np.concatenate([hi, hi, hi, mid, mid, lo], axis=1),
        two_parts(tangents.T),
    )
    return [np.ascontiguousarray(a, dtype=np.float32) for a in arrays]


def split_table(a):
    parts, rest = [], a
    for _ in range(3):
        part = rest.astype(ml_dtypes.bfloat16).astype(np.float64)
        parts.append(part)
        rest = rest - part
    return parts


def two_parts(a):
    hi, mid, _ = split_table(a)
    return np.concatenate([hi, mid, hi], axis=1)


def split(x, count):
    parts = []
    for _ in range(count - 1):
        part = x.astype(BF16).astype(F32)
        parts.append(part)
        x = x - part
    return parts + [x]


def rows_of(parts):
    return jnp.concatenate(parts, axis=0).astype(BF16)


def apply_table(table, data):
    hi, lo = split(data, 2)
    return jnp.dot(table, rows_of([hi, hi, lo]), preferred_element_type=F32)


def pick(data, hot):
    count = data.shape[0]
    out = jnp.dot(rows_of(split(data, 3)), hot, preferred_element_type=F32)
    return out[:count] + out[count:2 * count] + out[2 * count:]


def pick_t(data, hot):
    count = data.shape[0]
    out = lax.dot_general(
        rows_of(split(data, 3)), hot, (((1,), (1,)), ((), ())), preferred_element_type=F32
    )
    return out[:count] + out[count:2 * count] + out[2 * count:]


def cross(a, b):
    return [
        a[1] * b[2] - a[2] * b[1],
        a[2] * b[0] - a[0] * b[2],
        a[0] * b[1] - a[1] * b[0],
    ]


def dot3(a, b):
    return a[0] * b[0] + a[1] * b[1] + a[2] * b[2]


class Gas:
    def __init__(self, values):
        self.u, self.m = values, values[1:4]
        self.inv = 1.0 / values[0]
        self.v = [m * self.inv for m in self.m]
        self.p = 0.4 * (values[4] - 0.5 * dot3(self.m, self.v))
        self.h = values[4] + self.p

    def vary(self, tangent):
        self.du, self.dm = tangent, tangent[1:4]
        self.dv = [(self.dm[i] - self.v[i] * tangent[0]) * self.inv for i in range(3)]
        self.dp = 0.4 * (tangent[4] - 0.5 * (dot3(self.dm, self.v) + dot3(self.m, self.dv)))
        self.dh = tangent[4] + self.dp

    def along(self, n):
        vn = dot3(self.v, n)
        return [dot3(self.m, n)] + [self.m[k] * vn + self.p * n[k] for k in range(3)] + [self.h * vn]

    def along_change(self, n):
        vn, dvn = dot3(self.v, n), dot3(self.dv, n)
        middle = [self.dm[k] * vn + self.m[k] * dvn + self.dp * n[k] for k in range(3)]
        return [dot3(self.dm, n)] + middle + [self.dh * vn + self.h * dvn]

    def against(self, y):
        common = y[1] * self.m[0] + y[2] * self.m[1] + y[3] * self.m[2] + y[4] * self.h
        return [y[0] * self.m[i] + self.v[i] * common + y[1 + i] * self.p for i in range(3)]

    def speed(self, n, square, size):
        a = dot3(self.v, n)
        root = jnp.sqrt(a * a + SOFT * square)
        self.sound = jnp.sqrt(1.4 * self.p * self.inv)
        inv_root = 1.0 / root
        self.slope = a * inv_root
        sn = SOFT * inv_root + self.sound / size
        return root + self.sound * size, [self.slope * self.v[i] + sn * n[i] for i in range(3)]

    def speed_change(self, n, size):
        dsound = 0.7 * (self.dp - self.p * self.du[0] * self.inv) * self.inv / self.sound
        return self.slope * dot3(self.dv, n) + dsound * size


def kernel(n, group, *refs):
    sources, refs = refs[:INPUTS], refs[INPUTS:]
    results, refs = refs[:3], refs[3:]
    held, refs = refs[:INPUTS], refs[INPUTS:]
    (res_ref, change_ref, update_ref), refs = refs[:3], refs[3:]
    (state_ref, tangent_ref, far_ref, place_ref, damp_ref, neigh_ref, nodes_ref, upper_ref, lower_ref,
     sends_ref, flag_ref, select_ref, asm_ref, asm_t_ref, geo_ref, geo_t_ref) = held
    (up_out, up_in, down_out, down_in, place_out, place_in,
     gup_out, gup_in, gdown_out, gdown_in, sum_out, sum_in, send_sem, recv_sem, load_sem) = refs
    loads = [
        pltpu.make_async_copy(sources[i], held[i], load_sem.at[i]) for i in range(INPUTS)
    ]
    stores = [
        pltpu.make_async_copy(source, results[i], load_sem.at[INPUTS + i])
        for i, source in enumerate((res_ref, change_ref, update_ref))
    ]
    for i in LOAD_ORDER:
        loads[i].start()
    me = lax.axis_index("parts")
    right, left = lax.rem(me + 1, n), lax.rem(me + n - 1, n)
    elements = state_ref.shape[2]
    slots = upper_ref.shape[1]
    owned = place_ref.shape[1]
    shared = sends_ref.shape[1]
    own_pad = -(-owned // LANES) * LANES
    halo_pad = -(-shared // LANES) * LANES
    wide = 2 * elements

    stages = []
    low = 1
    while low < n:
        size = min(group, n // low)
        stages.append([low * k for k in range(1, size)])
        low *= size
    masks = [m for stage in stages for m in stage]

    def partner(mask):
        bit = me // mask % 2 if mask & (mask - 1) == 0 else None
        if bit is not None:
            return me + mask * (1 - 2 * bit)
        result = me
        b = 1
        while b <= mask:
            if mask & b:
                result = result + b * (1 - 2 * (me // b % 2))
            b *= 2
        return result

    partners = [partner(m) for m in masks]

    def remote(index, src, dst, device):
        return pltpu.make_async_remote_copy(
            src_ref=src, dst_ref=dst, send_sem=send_sem.at[index], recv_sem=recv_sem.at[index],
            device_id=(device,), device_id_type=MESH,
        )

    barrier = pltpu.get_barrier_semaphore()
    for device in [left, right] + partners:
        pl.semaphore_signal(barrier, inc=1, device_id=(device,), device_id_type=MESH)

    for i in LOAD_ORDER[:6]:
        loads[i].wait()
    own_rows = lax.broadcasted_iota(jnp.int32, (own_pad, halo_pad), 0)
    sends = sends_ref[...]
    if halo_pad > shared:
        sends = jnp.concatenate([sends, jnp.full((1, halo_pad - shared), -1, jnp.int32)], axis=1)
    sent_nodes = jnp.where(own_rows == sends, 1.0, 0.0).astype(BF16)
    places = jnp.zeros((8, own_pad), F32)
    place = place_ref[...]
    if own_pad > owned:
        place = jnp.concatenate([place, jnp.zeros((3, own_pad - owned), F32)], axis=1)
    places = jnp.concatenate([place, jnp.zeros((5, own_pad), F32)], axis=0)
    place_out[...] = pick(places, sent_nodes)

    row = lax.broadcasted_iota(jnp.int32, (wide, wide), 0)
    in_tangent = row >= elements
    local_key = jnp.where(in_tangent, row - elements + OTHER, row)
    slot = jnp.where(in_tangent, row - elements, row)
    halo_key = jnp.where(slot < slots, local_key + elements, -1)

    def one_hot(key, index):
        return jnp.where(key == index, 1.0, 0.0).astype(BF16)

    def send_hot(index):
        if slots < elements:
            pad = jnp.full((1, elements - slots), -2, jnp.int32)
            index = jnp.concatenate([index, pad, index + OTHER, pad], axis=1)
        else:
            index = jnp.concatenate([index, index + OTHER], axis=1)
        return one_hot(local_key, index)

    values = [state_ref[v] for v in range(5)]
    tangent = [tangent_ref[v] for v in range(5)]
    both = [jnp.concatenate([values[v], tangent[v]], axis=1) for v in range(5)]
    top = POINTS - FACE
    up_out[...] = pick(
        jnp.concatenate([both[v][top:POINTS] for v in range(5)], axis=0), send_hot(upper_ref[...])
    )
    down_out[...] = pick(
        jnp.concatenate([both[v][0:FACE] for v in range(5)], axis=0), send_hot(lower_ref[...])
    )
    pl.semaphore_wait(barrier, 2 + len(partners))
    place_copy = remote(0, place_out, place_in, left)
    up_copy = remote(1, up_out, up_in, right)
    down_copy = remote(2, down_out, down_in, left)
    place_copy.start()
    up_copy.start()
    down_copy.start()

    for i in LOAD_ORDER[6:]:
        loads[i].wait()
    weight = flag_ref[...].astype(F32)
    far_field = far_ref[...]
    damping = damp_ref[...]
    gas = Gas(values)
    select = select_ref[...].astype(BF16)
    traces = jnp.dot(
        select, rows_of(split(jnp.concatenate(both, axis=1), 3)), preferred_element_type=F32
    )
    trace = [traces[:, v * wide:(v + 1) * wide] for v in range(5)]
    neigh = neigh_ref[...]
    neigh = jnp.concatenate([neigh, neigh + OTHER], axis=1)
    far = jnp.where(neigh == elements + slots, 1.0, 0.0).astype(F32)
    outer = []
    for f in range(6):
        opposite = FACE * (f ^ 1)
        stack = jnp.concatenate([trace[v][opposite:opposite + FACE] for v in range(5)], axis=0)
        found = pick(stack, one_hot(local_key, neigh[f:f + 1]))
        outer.append(found)
    nodes = nodes_ref[...]
    nodes = jnp.where(nodes >= owned, nodes + (own_pad - owned), nodes)
    nodes = jnp.concatenate([nodes[k:k + 1] for k in range(8)], axis=1)
    table_rows = lax.broadcasted_iota(jnp.int32, (own_pad + halo_pad, 8 * elements), 0)
    corner_hot = one_hot(table_rows, nodes)

    def corners_of(table):
        found = pick(table, corner_hot)
        return [
            jnp.concatenate(
                [found[i:i + 1, k * elements:(k + 1) * elements] for k in range(8)], axis=0
            )
            for i in range(3)
        ]

    geo = geo_ref[...].astype(BF16)

    def edges_of(corners):
        hi, mid, lo = split(jnp.concatenate(corners, axis=1), 3)
        out = jnp.dot(geo, rows_of([hi, mid, lo, hi, mid, hi]), preferred_element_type=F32)
        rows = [out[:, i * elements:(i + 1) * elements] for i in range(3)]
        volume = [[rows[i][POINTS * j:POINTS * (j + 1)] for i in range(3)] for j in range(3)]
        base = 3 * POINTS
        first = [rows[i][base:base + 6 * FACE] for i in range(3)]
        second = [rows[i][base + 6 * FACE:base + 12 * FACE] for i in range(3)]
        lap = [rows[i][base + 12 * FACE:] for i in range(3)]
        return volume, first, second, lap

    place_copy.wait()
    corners = corners_of(jnp.concatenate([places, place_in[...]], axis=1))
    edge, first, second, lap = edges_of(corners)
    normals = [cross(edge[(j + 1) % 3], edge[(j + 2) % 3]) for j in range(3)]
    face_n = cross(first, second)
    square = dot3(face_n, face_n)
    size = jnp.sqrt(square)

    flux = [gas.along(normals[j]) for j in range(3)]
    inner = Gas([t[:, :elements] for t in trace])
    inner_speed, inner_grad = inner.speed(face_n, square, size)

    up_copy.wait()
    outer[0] = outer[0] + pick(up_in[...], one_hot(halo_key, neigh[0:1]))
    down_copy.wait()
    outer[1] = outer[1] + pick(down_in[...], one_hot(halo_key, neigh[1:2]))
    side = []
    for v in range(5):
        side.append(
            jnp.concatenate(
                [
                    outer[f][FACE * v:FACE * (v + 1)] + far[f:f + 1] * far_field[:, v:v + 1]
                    for f in range(6)
                ],
                axis=0,
            )
        )
    other = Gas([t[:, :elements] for t in side])
    other_speed, other_grad = other.speed(face_n, square, size)
    gap = inner_speed - other_speed
    root = jnp.sqrt(gap * gap + SOFT * square)
    inv_root = 0.5 / root
    lam = 0.5 * (inner_speed + other_speed) + 0.5 * root
    lam_n = [
        0.5 * (inner_grad[i] + other_grad[i])
        + (gap * (inner_grad[i] - other_grad[i]) + SOFT * face_n[i]) * inv_root
        for i in range(3)
    ]
    diff = [other.u[v] - inner.u[v] for v in range(5)]
    inner_along, other_along = inner.along(face_n), other.along(face_n)
    asm = asm_ref[...].astype(BF16)
    columns = []
    for v in range(5):
        jump = 0.5 * (other_along[v] - inner_along[v] - lam * diff[v])
        columns.append(jnp.concatenate([flux[0][v], flux[1][v], flux[2][v], jump], axis=0))
    result = apply_table(asm, jnp.concatenate(columns, axis=1))
    weighted = []
    for v in range(5):
        residual = result[:, v * elements:(v + 1) * elements]
        res_ref[v] = residual
        weighted.append(residual * weight)
    stores[0].start()

    asm_t = asm_t_ref[...].astype(BF16)
    back = [apply_table(asm_t, weighted[v]) for v in range(5)]
    grads = [gas.against([b[POINTS * j:POINTS * (j + 1)] for b in back]) for j in range(3)]
    face_back = [b[3 * POINTS:] for b in back]
    across = sum(face_back[v] * diff[v] for v in range(5))
    inner_against, other_against = inner.against(face_back), other.against(face_back)
    face_grad = [
        0.5 * (other_against[i] - inner_against[i] - across * lam_n[i]) for i in range(3)
    ]
    edge_grad = []
    for j in range(3):
        one = cross(edge[(j + 1) % 3], grads[(j + 2) % 3])
        two = cross(grads[(j + 1) % 3], edge[(j + 2) % 3])
        edge_grad.append([one[i] + two[i] for i in range(3)])
    first_grad, second_grad = cross(second, face_grad), cross(face_grad, first)
    smoothing = damping[:, 1:2]
    geo_t = geo_t_ref[...].astype(BF16)
    stack = [
        jnp.concatenate(
            [edge_grad[0][i], edge_grad[1][i], edge_grad[2][i], first_grad[i], second_grad[i]], axis=0
        )
        for i in range(3)
    ]
    pulled = apply_table(geo_t, jnp.concatenate(stack, axis=1))
    rows = []
    for i in range(3):
        corner_grad = pulled[:, i * elements:(i + 1) * elements] + smoothing * weight * lap[i]
        rows.append(jnp.concatenate([corner_grad[k:k + 1] for k in range(8)], axis=1))
    rows.append(jnp.concatenate([weight] * 8, axis=1))
    rows.append(jnp.zeros((4, 8 * elements), F32))
    table = pick_t(jnp.concatenate(rows, axis=0), corner_hot)
    own_part, halo_part = table[:, :own_pad], table[:, own_pad:]

    gup_out[...] = halo_part
    gup_copy = remote(3, gup_out, gup_in, right)
    gup_copy.start()
    gdown_out[...] = pick(own_part, sent_nodes)
    gdown_copy = remote(4, gdown_out, gdown_in, left)
    gdown_copy.start()

    gas.vary(tangent)
    inner.vary([t[:, elements:] for t in trace])
    other.vary([t[:, elements:] for t in side])
    flux_change = [gas.along_change(normals[j]) for j in range(3)]
    inner_dspeed, other_dspeed = inner.speed_change(face_n, size), other.speed_change(face_n, size)
    dlam = 0.5 * (inner_dspeed + other_dspeed) + gap * (inner_dspeed - other_dspeed) * inv_root
    inner_change, other_change = inner.along_change(face_n), other.along_change(face_n)
    columns = []
    for v in range(5):
        ddiff = other.du[v] - inner.du[v]
        djump = 0.5 * (other_change[v] - inner_change[v] - dlam * diff[v] - lam * ddiff)
        columns.append(
            jnp.concatenate([flux_change[0][v], flux_change[1][v], flux_change[2][v], djump], axis=0)
        )
    result = apply_table(asm, jnp.concatenate(columns, axis=1))
    for v in range(5):
        change_ref[v] = result[:, v * elements:(v + 1) * elements]
    stores[1].start()

    def descent_of(total):
        line = lax.broadcasted_iota(jnp.int32, total.shape, 0)
        touched = jnp.where(total[3:4] > 0.5, 1.0, 0.0)
        return -jnp.where(line < 3, total * touched, 0.0)

    gup_copy.wait()
    descent = descent_of(own_part + pick_t(gup_in[...], sent_nodes))
    gdown_copy.wait()
    halo_descent = descent_of(halo_part + gdown_in[...])

    steps = corners_of(jnp.concatenate([descent, halo_descent], axis=1))
    dedge, dfirst, dsecond, dlap = edges_of(steps)
    dflux = []
    for j in range(3):
        a, b = (j + 1) % 3, (j + 2) % 3
        one, two = cross(dedge[a], edge[b]), cross(edge[a], dedge[b])
        dflux.append(gas.along([one[i] + two[i] for i in range(3)]))
    one, two = cross(dfirst, second), cross(first, dsecond)
    dface = [one[i] + two[i] for i in range(3)]
    inner_dalong, other_dalong = inner.along(dface), other.along(dface)
    dlam_n = dot3(lam_n, dface)
    columns = []
    for v in range(5):
        jump = 0.5 * (other_dalong[v] - inner_dalong[v] - dlam_n * diff[v])
        columns.append(jnp.concatenate([dflux[0][v], dflux[1][v], dflux[2][v], jump], axis=0))
    moved = apply_table(asm, jnp.concatenate(columns, axis=1))
    squares = jnp.sum(moved * moved, axis=0, keepdims=True)
    squares = sum(squares[:, v * elements:(v + 1) * elements] for v in range(5))
    curvature = squares * weight
    bent = sum(steps[i] * dlap[i] for i in range(3))
    bending = smoothing * jnp.sum(bent, axis=0, keepdims=True) * weight
    norm = jnp.sum(descent * descent, axis=0, keepdims=True)
    both_sums = jnp.sum(curvature + bending, axis=1, keepdims=True)
    norm_sum = jnp.sum(norm, axis=1, keepdims=True)
    line = lax.broadcasted_iota(jnp.int32, (8, LANES), 0)
    sums = jnp.where(line == 0, norm_sum, jnp.where(line == 1, both_sums, 0.0))

    index = 0
    for s, stage in enumerate(stages):
        sum_out[s] = sums
        copies = []
        for _ in stage:
            copies.append(remote(5 + index, sum_out.at[s], sum_in.at[index], partners[index]))
            copies[-1].start()
            index += 1
        for i, copy in enumerate(copies):
            copy.wait_recv()
        for i in range(len(stage)):
            sums = sums + sum_in[index - len(stage) + i]
        for copy in copies:
            copy.wait_send()
    norm_total, rest = sums[0:1, 0:1], sums[1:2, 0:1]
    step_size = norm_total / (rest + damping[:, 0:1] * norm_total)
    update_ref[...] = (descent * step_size)[0:3, :owned]
    stores[2].start()
    for store in stores:
        store.wait()


def write_out(*refs):
    loads = [pltpu.make_async_copy(refs[i], refs[6 + i], refs[9].at[i]) for i in range(3)]
    stores = [pltpu.make_async_copy(refs[6 + i], refs[3 + i], refs[9].at[3 + i]) for i in range(3)]
    for load in loads:
        load.start()
    for load, store in zip(loads, stores):
        load.wait()
        store.start()
    for store in stores:
        store.wait()


def body(n, group, flow_state, state_tangent, far_field, coordinates, damping, face_neighbour,
         element_nodes, upper_sends, lower_sends, node_sends, shock_flags):
    own_pad = -(-coordinates.shape[1] // LANES) * LANES
    halo_pad = -(-node_sends.shape[0] // LANES) * LANES
    wide = 2 * flow_state.shape[2]
    count, stages, low = 0, 0, 1
    while low < n:
        size = min(group, n // low)
        count, stages, low = count + size - 1, stages + 1, low * size
    hbm = pl.BlockSpec(memory_space=pltpu.HBM)
    constants = [jnp.asarray(t) for t in tables()]
    halo = pltpu.VMEM((5 * FACE, wide), F32)
    place = pltpu.VMEM((8, halo_pad), F32)
    operands = [
        flow_state, state_tangent, far_field.reshape(1, -1), coordinates, damping.reshape(1, -1),
        face_neighbour, element_nodes,
        upper_sends.reshape(1, -1), lower_sends.reshape(1, -1), node_sends.reshape(1, -1),
        shock_flags.reshape(1, -1),
    ] + constants
    shapes = (
        jax.ShapeDtypeStruct(flow_state.shape, F32),
        jax.ShapeDtypeStruct(flow_state.shape, F32),
        jax.ShapeDtypeStruct(coordinates.shape, F32),
    )
    results = pl.pallas_call(
        functools.partial(kernel, n, group),
        out_shape=shapes,
        in_specs=[hbm] * len(operands),
        out_specs=(hbm, hbm, hbm),
        scratch_shapes=[pltpu.VMEM(o.shape, o.dtype) for o in operands + list(shapes)] + [halo] * 4 + [place] * 6 + [
            pltpu.VMEM((stages, 8, LANES), F32),
            pltpu.VMEM((count, 8, LANES), F32),
            pltpu.SemaphoreType.DMA((5 + count,)),
            pltpu.SemaphoreType.DMA((5 + count,)),
            pltpu.SemaphoreType.DMA((INPUTS + 3,)),
        ],
        compiler_params=pltpu.CompilerParams(
            collective_id=0, has_side_effects=True, vmem_limit_bytes=VMEM_LIMIT
        ),
    )(*operands)
    return pl.pallas_call(
        write_out,
        out_shape=shapes,
        in_specs=[hbm] * 3,
        out_specs=[hbm] * 3,
        scratch_shapes=[pltpu.VMEM(o.shape, o.dtype) for o in shapes] + [pltpu.SemaphoreType.DMA((6,))],
        compiler_params=pltpu.CompilerParams(vmem_limit_bytes=VMEM_LIMIT),
    )(*results)


def solution(mesh):
    n = mesh.shape["parts"]
    in_specs = (
        P(None, None, "parts"),
        P(None, None, "parts"),
        P(),
        P(None, "parts"),
        P(),
        P(None, "parts"),
        P(None, "parts"),
        P("parts"),
        P("parts"),
        P("parts"),
        P("parts"),
    )
    out_specs = (P(None, None, "parts"), P(None, None, "parts"), P(None, "parts"))
    return jax.shard_map(
        functools.partial(body, n, 8), mesh=mesh, in_specs=in_specs, out_specs=out_specs,
        check_vma=False,
    )
```

```python
import functools
import math

import jax
import jax.numpy as jnp
import ml_dtypes
import numpy as np
from jax import lax
from jax.experimental import pallas as pl
from jax.experimental.pallas import tpu as pltpu
from jax.sharding import PartitionSpec as P

SOFT = 0.01
MESH = pl.DeviceIdType.MESH
F32 = jnp.float32
BF16 = jnp.bfloat16
OTHER = 4096
FACE = 16
POINTS = 64
INPUTS = 16
ROWS = 8
GEO = 12 * FACE + 3 * POINTS + 8
VMEM_LIMIT = 60 * 1024 * 1024
LOAD_ORDER = (9, 3, 7, 8, 0, 1, 11, 5, 6, 14, 2, 4, 10, 12, 13, 15)
LANES = 128


def lobatto_tables():
    points = np.array([-1.0, -math.sqrt(0.2), math.sqrt(0.2), 1.0])
    weights = np.array([1.0, 5.0, 5.0, 1.0]) / 6.0
    derivative = np.zeros((4, 4))
    for a in range(4):
        for b in range(4):
            if a == b:
                derivative[a, b] = sum((1.0 / (points[a] - points[m]) for m in range(4) if m != a))
            else:
                numerator = 1.0
                denominator = 1.0
                for m in range(4):
                    if m != b:
                        denominator *= points[b] - points[m]
                        if m != a:
                            numerator *= points[a] - points[m]
                derivative[a, b] = numerator / denominator
    return (points, weights, derivative)


def shape_gradients():
    points = lobatto_tables()[0]
    gradients = np.zeros((3, 64, 8))
    for q in range(64):
        position = (q // 16, q // 4 % 4, q % 4)
        for k in range(8):
            corner_bits = (k // 4, k // 2 % 2, k % 2)
            for j in range(3):
                factor = 1.0
                for m in range(3):
                    orient = 1.0 if corner_bits[m] == 1 else -1.0
                    if m == j:
                        factor *= 0.5 * orient
                    else:
                        factor *= 0.5 * (1.0 + orient * points[position[m]])
                gradients[j, q, k] = factor
    return gradients


def edge_laplacian():
    matrix = np.zeros((8, 8))
    for k in range(8):
        matrix[k, k] = 3.0
        for b in range(3):
            matrix[k, k ^ 1 << b] = -1.0
    return matrix


def tables():
    _, weights, derivative = lobatto_tables()
    gradients = shape_gradients()
    grid = np.arange(64).reshape(4, 4, 4)
    face_rows = [np.take(grid, 3 * (f % 2), axis=f // 2).reshape(-1) for f in range(6)]
    select = np.zeros((96, 64))
    select[np.arange(96), np.concatenate(face_rows)] = 1.0
    volume = (weights[:, None, None] * weights[None, :, None] * weights[None, None, :]).reshape(-1)
    face_weights = np.tile((weights[:, None] * weights[None, :]).reshape(-1), 6)
    eye = np.eye(4)
    applied = [
        np.kron(derivative, np.kron(eye, eye)),
        np.kron(eye, np.kron(derivative, eye)),
        np.kron(eye, np.kron(eye, derivative)),
    ]
    assembly = np.concatenate(
        [volume[:, None] * m for m in applied] + [select.T * face_weights[None, :]], axis=1
    )
    first = [gradients[(f // 2 + 1) % 3][face_rows[f]] * (2.0 * (f % 2) - 1.0) for f in range(6)]
    second = [gradients[(f // 2 + 2) % 3][face_rows[f]] for f in range(6)]
    tangents = np.concatenate([gradients.reshape(192, 8)] + first + second, axis=0)
    hi, mid, lo = split_table(np.concatenate([tangents, edge_laplacian()], axis=0))
    arrays = (
        np.concatenate([select] * 3, axis=1),
        two_parts(assembly),
        two_parts(assembly.T),
        np.concatenate([hi, hi, hi, mid, mid, lo], axis=1),
        two_parts(tangents.T),
    )
    return [np.ascontiguousarray(a, dtype=np.float32) for a in arrays]


def split_table(a):
    parts, rest = [], a
    for _ in range(3):
        part = rest.astype(ml_dtypes.bfloat16).astype(np.float64)
        parts.append(part)
        rest = rest - part
    return parts


def two_parts(a):
    hi, mid, _ = split_table(a)
    return np.concatenate([hi, mid, hi], axis=1)


def split(x, count):
    parts = []
    for _ in range(count - 1):
        part = x.astype(BF16).astype(F32)
        parts.append(part)
        x = x - part
    return parts + [x]


def rows_of(parts):
    return jnp.concatenate(parts, axis=0).astype(BF16)


def apply_table(table, data):
    hi, lo = split(data, 2)
    return jnp.dot(table, rows_of([hi, hi, lo]), preferred_element_type=F32)


def pick(data, hot):
    count = data.shape[0]
    out = jnp.dot(rows_of(split(data, 3)), hot, preferred_element_type=F32)
    return out[:count] + out[count:2 * count] + out[2 * count:]


def pick_t(data, hot):
    count = data.shape[0]
    out = lax.dot_general(
        rows_of(split(data, 3)), hot, (((1,), (1,)), ((), ())), preferred_element_type=F32
    )
    return out[:count] + out[count:2 * count] + out[2 * count:]


def cross(a, b):
    return [
        a[1] * b[2] - a[2] * b[1],
        a[2] * b[0] - a[0] * b[2],
        a[0] * b[1] - a[1] * b[0],
    ]


def dot3(a, b):
    return a[0] * b[0] + a[1] * b[1] + a[2] * b[2]


class Gas:
    def __init__(self, values, saved=None):
        self.u, self.m = values, values[1:4]
        if saved is not None:
            self.inv, self.p, self.h, *self.v = saved
            return
        self.inv = 1.0 / values[0]
        self.v = [m * self.inv for m in self.m]
        self.p = 0.4 * (values[4] - 0.5 * dot3(self.m, self.v))
        self.h = values[4] + self.p

    def saved(self):
        return [self.inv, self.p, self.h] + self.v

    def vary(self, tangent):
        self.du, self.dm = tangent, tangent[1:4]
        self.dv = [(self.dm[i] - self.v[i] * tangent[0]) * self.inv for i in range(3)]
        self.dp = 0.4 * (tangent[4] - 0.5 * (dot3(self.dm, self.v) + dot3(self.m, self.dv)))
        self.dh = tangent[4] + self.dp

    def along(self, n):
        vn = dot3(self.v, n)
        return [dot3(self.m, n)] + [self.m[k] * vn + self.p * n[k] for k in range(3)] + [self.h * vn]

    def along_change(self, n):
        vn, dvn = dot3(self.v, n), dot3(self.dv, n)
        middle = [self.dm[k] * vn + self.m[k] * dvn + self.dp * n[k] for k in range(3)]
        return [dot3(self.dm, n)] + middle + [self.dh * vn + self.h * dvn]

    def against(self, y):
        common = y[1] * self.m[0] + y[2] * self.m[1] + y[3] * self.m[2] + y[4] * self.h
        return [y[0] * self.m[i] + self.v[i] * common + y[1 + i] * self.p for i in range(3)]

    def speed(self, n, square, size):
        a = dot3(self.v, n)
        root = jnp.sqrt(a * a + SOFT * square)
        self.sound = jnp.sqrt(1.4 * self.p * self.inv)
        inv_root = 1.0 / root
        self.slope = a * inv_root
        sn = SOFT * inv_root + self.sound / size
        return root + self.sound * size, [self.slope * self.v[i] + sn * n[i] for i in range(3)]

    def speed_change(self, n, size):
        dsound = 0.7 * (self.dp - self.p * self.du[0] * self.inv) * self.inv / self.sound
        return self.slope * dot3(self.dv, n) + dsound * size


def chunks(count, step):
    def one(c, carry):
        step(pl.multiple_of(c * ROWS, ROWS))
        return carry

    lax.fori_loop(0, count // ROWS, one, 0, unroll=2)


def kernel(n, group, *refs):
    sources, refs = refs[:INPUTS], refs[INPUTS:]
    results, refs = refs[:3], refs[3:]
    held, refs = refs[:INPUTS], refs[INPUTS:]
    (res_ref, change_ref, update_ref), refs = refs[:3], refs[3:]
    (state_ref, tangent_ref, far_ref, place_ref, damp_ref, neigh_ref, nodes_ref, upper_ref, lower_ref,
     sends_ref, flag_ref, select_ref, asm_ref, asm_t_ref, geo_ref, geo_t_ref) = held
    (up_out, up_in, down_out, down_in, place_out, place_in,
     gup_out, gup_in, gdown_out, gdown_in, sum_out, sum_in, send_sem, recv_sem, load_sem,
     trace_s, side_s, geo_s, dgeo_s, vol_s, face_s, x_s, back_s, pull_s) = refs
    loads = [
        pltpu.make_async_copy(sources[i], held[i], load_sem.at[i]) for i in range(INPUTS)
    ]
    stores = [
        pltpu.make_async_copy(source, results[i], load_sem.at[INPUTS + i])
        for i, source in enumerate((res_ref, change_ref, update_ref))
    ]
    for i in LOAD_ORDER:
        loads[i].start()
    me = lax.axis_index("parts")
    right, left = lax.rem(me + 1, n), lax.rem(me + n - 1, n)
    elements = state_ref.shape[2]
    slots = upper_ref.shape[1]
    owned = place_ref.shape[1]
    shared = sends_ref.shape[1]
    own_pad = -(-owned // LANES) * LANES
    halo_pad = -(-shared // LANES) * LANES
    wide = 2 * elements

    stages = []
    low = 1
    while low < n:
        size = min(group, n // low)
        stages.append([low * k for k in range(1, size)])
        low *= size
    masks = [m for stage in stages for m in stage]

    def partner(mask):
        bit = me // mask % 2 if mask & (mask - 1) == 0 else None
        if bit is not None:
            return me + mask * (1 - 2 * bit)
        result = me
        b = 1
        while b <= mask:
            if mask & b:
                result = result + b * (1 - 2 * (me // b % 2))
            b *= 2
        return result

    partners = [partner(m) for m in masks]

    def remote(index, src, dst, device):
        return pltpu.make_async_remote_copy(
            src_ref=src, dst_ref=dst, send_sem=send_sem.at[index], recv_sem=recv_sem.at[index],
            device_id=(device,), device_id_type=MESH,
        )

    barrier = pltpu.get_barrier_semaphore()
    for device in [left, right] + partners:
        pl.semaphore_signal(barrier, inc=1, device_id=(device,), device_id_type=MESH)

    for i in LOAD_ORDER[:6]:
        loads[i].wait()
    own_rows = lax.broadcasted_iota(jnp.int32, (own_pad, halo_pad), 0)
    sends = sends_ref[...]
    if halo_pad > shared:
        sends = jnp.concatenate([sends, jnp.full((1, halo_pad - shared), -1, jnp.int32)], axis=1)
    sent_nodes = jnp.where(own_rows == sends, 1.0, 0.0).astype(BF16)
    places = jnp.zeros((8, own_pad), F32)
    place = place_ref[...]
    if own_pad > owned:
        place = jnp.concatenate([place, jnp.zeros((3, own_pad - owned), F32)], axis=1)
    places = jnp.concatenate([place, jnp.zeros((5, own_pad), F32)], axis=0)
    place_out[...] = pick(places, sent_nodes)

    row = lax.broadcasted_iota(jnp.int32, (wide, wide), 0)
    in_tangent = row >= elements
    local_key = jnp.where(in_tangent, row - elements + OTHER, row)
    slot = jnp.where(in_tangent, row - elements, row)
    halo_key = jnp.where(slot < slots, local_key + elements, -1)

    def one_hot(key, index):
        return jnp.where(key == index, 1.0, 0.0).astype(BF16)

    def send_hot(index):
        if slots < elements:
            pad = jnp.full((1, elements - slots), -2, jnp.int32)
            index = jnp.concatenate([index, pad, index + OTHER, pad], axis=1)
        else:
            index = jnp.concatenate([index, index + OTHER], axis=1)
        return one_hot(local_key, index)

    values = [state_ref[v] for v in range(5)]
    tangent = [tangent_ref[v] for v in range(5)]
    both = [jnp.concatenate([values[v], tangent[v]], axis=1) for v in range(5)]
    top = POINTS - FACE
    up_out[...] = pick(
        jnp.concatenate([both[v][top:POINTS] for v in range(5)], axis=0), send_hot(upper_ref[...])
    )
    down_out[...] = pick(
        jnp.concatenate([both[v][0:FACE] for v in range(5)], axis=0), send_hot(lower_ref[...])
    )
    pl.semaphore_wait(barrier, 2 + len(partners))
    place_copy = remote(0, place_out, place_in, left)
    up_copy = remote(1, up_out, up_in, right)
    down_copy = remote(2, down_out, down_in, left)
    place_copy.start()
    up_copy.start()
    down_copy.start()

    for i in LOAD_ORDER[6:]:
        loads[i].wait()
    weight = flag_ref[...].astype(F32)
    far_field = far_ref[...]
    damping = damp_ref[...]
    select = select_ref[...].astype(BF16)
    traces = jnp.dot(
        select, rows_of(split(jnp.concatenate(both, axis=1), 3)), preferred_element_type=F32
    )
    trace_s[...] = traces
    trace = [traces[:, v * wide:(v + 1) * wide] for v in range(5)]
    neigh = neigh_ref[...]
    neigh = jnp.concatenate([neigh, neigh + OTHER], axis=1)
    far = jnp.where(neigh == elements + slots, 1.0, 0.0).astype(F32)
    outer = []
    for f in range(6):
        opposite = FACE * (f ^ 1)
        stack = jnp.concatenate([trace[v][opposite:opposite + FACE] for v in range(5)], axis=0)
        found = pick(stack, one_hot(local_key, neigh[f:f + 1]))
        outer.append(found)
    nodes = nodes_ref[...]
    nodes = jnp.where(nodes >= owned, nodes + (own_pad - owned), nodes)
    nodes = jnp.concatenate([nodes[k:k + 1] for k in range(8)], axis=1)
    table_rows = lax.broadcasted_iota(jnp.int32, (own_pad + halo_pad, 8 * elements), 0)
    corner_hot = one_hot(table_rows, nodes)

    def corners_of(table):
        found = pick(table, corner_hot)
        return [
            jnp.concatenate(
                [found[i:i + 1, k * elements:(k + 1) * elements] for k in range(8)], axis=0
            )
            for i in range(3)
        ]

    geo = geo_ref[...].astype(BF16)

    def edges_of(corners, out):
        for i in range(3):
            hi, mid, lo = split(corners[i], 3)
            out[i] = jnp.dot(geo, rows_of([hi, mid, lo, hi, mid, hi]), preferred_element_type=F32)

    base = 3 * POINTS
    sides = 6 * FACE

    def volume_edges(source, r):
        return [[source[i, pl.ds(POINTS * j + r, ROWS)] for i in range(3)] for j in range(3)]

    def face_edges(source, r):
        first = [source[i, pl.ds(base + r, ROWS)] for i in range(3)]
        second = [source[i, pl.ds(base + sides + r, ROWS)] for i in range(3)]
        return first, second

    def put(target, r, values, at=0):
        for k, value in enumerate(values):
            target[at + k, pl.ds(r, ROWS)] = value

    def take(source, r, count, at=0):
        return [source[at + k, pl.ds(r, ROWS)] for k in range(count)]

    def lanes(source, r, tangent_half):
        at = elements if tangent_half else 0
        return [source[pl.ds(r, ROWS), v * wide + at:v * wide + at + elements] for v in range(5)]

    def volume_gas(r):
        return Gas(take(state_ref, r, 5), take(vol_s, r, 6))

    def face_gas(r):
        inner = Gas(lanes(trace_s, r, False), take(face_s, r, 6))
        other = Gas(lanes(side_s, r, False), take(face_s, r, 6, 6))
        return inner, other

    place_copy.wait()
    corners = corners_of(jnp.concatenate([places, place_in[...]], axis=1))
    edges_of(corners, geo_s)
    lap = [geo_s[i, base + 2 * sides:] for i in range(3)]

    def volume_flux(r):
        edge = volume_edges(geo_s, r)
        gas = Gas(take(state_ref, r, 5))
        put(vol_s, r, gas.saved())
        for j in range(3):
            normal = cross(edge[(j + 1) % 3], edge[(j + 2) % 3])
            put(vol_s, r, normal, 6 + 3 * j)
            put(x_s, POINTS * j + r, gas.along(normal))

    chunks(POINTS, volume_flux)

    up_copy.wait()
    outer[0] = outer[0] + pick(up_in[...], one_hot(halo_key, neigh[0:1]))
    down_copy.wait()
    outer[1] = outer[1] + pick(down_in[...], one_hot(halo_key, neigh[1:2]))
    for v in range(5):
        side_s[:, v * wide:(v + 1) * wide] = jnp.concatenate(
            [
                outer[f][FACE * v:FACE * (v + 1)] + far[f:f + 1] * far_field[:, v:v + 1]
                for f in range(6)
            ],
            axis=0,
        )

    def face_flux(r):
        face_n = cross(*face_edges(geo_s, r))
        square = dot3(face_n, face_n)
        size = jnp.sqrt(square)
        inner, other = Gas(lanes(trace_s, r, False)), Gas(lanes(side_s, r, False))
        inner_speed, inner_grad = inner.speed(face_n, square, size)
        other_speed, other_grad = other.speed(face_n, square, size)
        gap = inner_speed - other_speed
        root = jnp.sqrt(gap * gap + SOFT * square)
        inv_root = 0.5 / root
        lam = 0.5 * (inner_speed + other_speed) + 0.5 * root
        lam_n = [
            0.5 * (inner_grad[i] + other_grad[i])
            + (gap * (inner_grad[i] - other_grad[i]) + SOFT * face_n[i]) * inv_root
            for i in range(3)
        ]
        one, two = inner.along(face_n), other.along(face_n)
        jump = [0.5 * (two[v] - one[v] - lam * (other.u[v] - inner.u[v])) for v in range(5)]
        put(x_s, base + r, jump)
        put(face_s, r, inner.saved() + other.saved() + face_n + lam_n)
        rest = [size, lam, gap * inv_root, inner.slope, inner.sound, other.slope, other.sound]
        put(face_s, r, rest, 18)

    chunks(sides, face_flux)
    asm = asm_ref[...].astype(BF16)

    def assembled():
        return apply_table(asm, jnp.concatenate([x_s[v] for v in range(5)], axis=1))

    result = assembled()
    weighted = []
    for v in range(5):
        residual = result[:, v * elements:(v + 1) * elements]
        res_ref[v] = residual
        weighted.append(residual * weight)
    stores[0].start()

    asm_t = asm_t_ref[...].astype(BF16)
    for v in range(5):
        back_s[v] = apply_table(asm_t, weighted[v])

    def volume_pull(r):
        edge = volume_edges(geo_s, r)
        gas = volume_gas(r)
        grads = [gas.against(take(back_s, POINTS * j + r, 5)) for j in range(3)]
        for j in range(3):
            one = cross(edge[(j + 1) % 3], grads[(j + 2) % 3])
            two = cross(grads[(j + 1) % 3], edge[(j + 2) % 3])
            put(pull_s, POINTS * j + r, [one[i] + two[i] for i in range(3)])

    def face_pull(r):
        first, second = face_edges(geo_s, r)
        inner, other = face_gas(r)
        lam_n = take(face_s, r, 3, 15)
        y = take(back_s, base + r, 5)
        across = sum(y[v] * (other.u[v] - inner.u[v]) for v in range(5))
        one, two = inner.against(y), other.against(y)
        grad = [0.5 * (two[i] - one[i] - across * lam_n[i]) for i in range(3)]
        put(pull_s, base + r, cross(second, grad))
        put(pull_s, base + sides + r, cross(grad, first))

    chunks(POINTS, volume_pull)
    chunks(sides, face_pull)
    smoothing = damping[:, 1:2]
    geo_t = geo_t_ref[...].astype(BF16)
    pulled = apply_table(geo_t, jnp.concatenate([pull_s[i] for i in range(3)], axis=1))
    rows = []
    for i in range(3):
        corner_grad = pulled[:, i * elements:(i + 1) * elements] + smoothing * weight * lap[i]
        rows.append(jnp.concatenate([corner_grad[k:k + 1] for k in range(8)], axis=1))
    rows.append(jnp.concatenate([weight] * 8, axis=1))
    rows.append(jnp.zeros((4, 8 * elements), F32))
    table = pick_t(jnp.concatenate(rows, axis=0), corner_hot)
    own_part, halo_part = table[:, :own_pad], table[:, own_pad:]

    gup_out[...] = halo_part
    gup_copy = remote(3, gup_out, gup_in, right)
    gup_copy.start()
    gdown_out[...] = pick(own_part, sent_nodes)
    gdown_copy = remote(4, gdown_out, gdown_in, left)
    gdown_copy.start()

    def volume_change(r):
        gas = volume_gas(r)
        gas.vary(take(tangent_ref, r, 5))
        for j in range(3):
            put(x_s, POINTS * j + r, gas.along_change(take(vol_s, r, 3, 6 + 3 * j)))

    def face_change(r):
        inner, other = face_gas(r)
        inner.vary(lanes(trace_s, r, True))
        other.vary(lanes(side_s, r, True))
        face_n = take(face_s, r, 3, 12)
        size, lam, lean, inner.slope, inner.sound, other.slope, other.sound = take(face_s, r, 7, 18)
        ds, dt = inner.speed_change(face_n, size), other.speed_change(face_n, size)
        dlam = 0.5 * (ds + dt) + lean * (ds - dt)
        one, two = inner.along_change(face_n), other.along_change(face_n)
        jump = []
        for v in range(5):
            moved = dlam * (other.u[v] - inner.u[v]) + lam * (other.du[v] - inner.du[v])
            jump.append(0.5 * (two[v] - one[v] - moved))
        put(x_s, base + r, jump)

    chunks(POINTS, volume_change)
    chunks(sides, face_change)
    result = assembled()
    for v in range(5):
        change_ref[v] = result[:, v * elements:(v + 1) * elements]
    stores[1].start()

    def descent_of(total):
        line = lax.broadcasted_iota(jnp.int32, total.shape, 0)
        touched = jnp.where(total[3:4] > 0.5, 1.0, 0.0)
        return -jnp.where(line < 3, total * touched, 0.0)

    gup_copy.wait()
    descent = descent_of(own_part + pick_t(gup_in[...], sent_nodes))
    gdown_copy.wait()
    halo_descent = descent_of(halo_part + gdown_in[...])

    steps = corners_of(jnp.concatenate([descent, halo_descent], axis=1))
    edges_of(steps, dgeo_s)
    dlap = [dgeo_s[i, base + 2 * sides:] for i in range(3)]

    def volume_step(r):
        edge, dedge = volume_edges(geo_s, r), volume_edges(dgeo_s, r)
        gas = volume_gas(r)
        for j in range(3):
            a, b = (j + 1) % 3, (j + 2) % 3
            one, two = cross(dedge[a], edge[b]), cross(edge[a], dedge[b])
            put(x_s, POINTS * j + r, gas.along([one[i] + two[i] for i in range(3)]))

    def face_step(r):
        first, second = face_edges(geo_s, r)
        dfirst, dsecond = face_edges(dgeo_s, r)
        inner, other = face_gas(r)
        one, two = cross(dfirst, second), cross(first, dsecond)
        dface = [one[i] + two[i] for i in range(3)]
        dlam = dot3(take(face_s, r, 3, 15), dface)
        one, two = inner.along(dface), other.along(dface)
        jump = [0.5 * (two[v] - one[v] - dlam * (other.u[v] - inner.u[v])) for v in range(5)]
        put(x_s, base + r, jump)

    chunks(POINTS, volume_step)
    chunks(sides, face_step)
    moved = assembled()
    squares = jnp.sum(moved * moved, axis=0, keepdims=True)
    squares = sum(squares[:, v * elements:(v + 1) * elements] for v in range(5))
    curvature = squares * weight
    bent = sum(steps[i] * dlap[i] for i in range(3))
    bending = smoothing * jnp.sum(bent, axis=0, keepdims=True) * weight
    norm = jnp.sum(descent * descent, axis=0, keepdims=True)
    both_sums = jnp.sum(curvature + bending, axis=1, keepdims=True)
    norm_sum = jnp.sum(norm, axis=1, keepdims=True)
    line = lax.broadcasted_iota(jnp.int32, (8, LANES), 0)
    sums = jnp.where(line == 0, norm_sum, jnp.where(line == 1, both_sums, 0.0))

    index = 0
    for s, stage in enumerate(stages):
        sum_out[s] = sums
        copies = []
        for _ in stage:
            copies.append(remote(5 + index, sum_out.at[s], sum_in.at[index], partners[index]))
            copies[-1].start()
            index += 1
        for i, copy in enumerate(copies):
            copy.wait_recv()
        for i in range(len(stage)):
            sums = sums + sum_in[index - len(stage) + i]
        for copy in copies:
            copy.wait_send()
    norm_total, rest = sums[0:1, 0:1], sums[1:2, 0:1]
    step_size = norm_total / (rest + damping[:, 0:1] * norm_total)
    update_ref[...] = (descent * step_size)[0:3, :owned]
    stores[2].start()
    for store in stores:
        store.wait()


def write_out(*refs):
    loads = [pltpu.make_async_copy(refs[i], refs[6 + i], refs[9].at[i]) for i in range(3)]
    stores = [pltpu.make_async_copy(refs[6 + i], refs[3 + i], refs[9].at[3 + i]) for i in range(3)]
    for load in loads:
        load.start()
    for load, store in zip(loads, stores):
        load.wait()
        store.start()
    for store in stores:
        store.wait()


def body(n, group, flow_state, state_tangent, far_field, coordinates, damping, face_neighbour,
         element_nodes, upper_sends, lower_sends, node_sends, shock_flags):
    own_pad = -(-coordinates.shape[1] // LANES) * LANES
    halo_pad = -(-node_sends.shape[0] // LANES) * LANES
    wide = 2 * flow_state.shape[2]
    count, stages, low = 0, 0, 1
    while low < n:
        size = min(group, n // low)
        count, stages, low = count + size - 1, stages + 1, low * size
    hbm = pl.BlockSpec(memory_space=pltpu.HBM)
    constants = [jnp.asarray(t) for t in tables()]
    halo = pltpu.VMEM((5 * FACE, wide), F32)
    place = pltpu.VMEM((8, halo_pad), F32)
    operands = [
        flow_state, state_tangent, far_field.reshape(1, -1), coordinates, damping.reshape(1, -1),
        face_neighbour, element_nodes,
        upper_sends.reshape(1, -1), lower_sends.reshape(1, -1), node_sends.reshape(1, -1),
        shock_flags.reshape(1, -1),
    ] + constants
    shapes = (
        jax.ShapeDtypeStruct(flow_state.shape, F32),
        jax.ShapeDtypeStruct(flow_state.shape, F32),
        jax.ShapeDtypeStruct(coordinates.shape, F32),
    )
    results = pl.pallas_call(
        functools.partial(kernel, n, group),
        out_shape=shapes,
        in_specs=[hbm] * len(operands),
        out_specs=(hbm, hbm, hbm),
        scratch_shapes=[pltpu.VMEM(o.shape, o.dtype) for o in operands + list(shapes)] + [halo] * 4 + [place] * 6 + [
            pltpu.VMEM((stages, 8, LANES), F32),
            pltpu.VMEM((count, 8, LANES), F32),
            pltpu.SemaphoreType.DMA((5 + count,)),
            pltpu.SemaphoreType.DMA((5 + count,)),
            pltpu.SemaphoreType.DMA((INPUTS + 3,)),
            pltpu.VMEM((6 * FACE, 5 * wide), F32),
            pltpu.VMEM((6 * FACE, 5 * wide), F32),
            pltpu.VMEM((3, GEO, wide // 2), F32),
            pltpu.VMEM((3, GEO, wide // 2), F32),
            pltpu.VMEM((15, POINTS, wide // 2), F32),
            pltpu.VMEM((25, 6 * FACE, wide // 2), F32),
            pltpu.VMEM((5, 3 * POINTS + 6 * FACE, wide // 2), F32),
            pltpu.VMEM((5, 3 * POINTS + 6 * FACE, wide // 2), F32),
            pltpu.VMEM((3, 3 * POINTS + 12 * FACE, wide // 2), F32),
        ],
        compiler_params=pltpu.CompilerParams(
            collective_id=0, has_side_effects=True, vmem_limit_bytes=VMEM_LIMIT
        ),
    )(*operands)
    return pl.pallas_call(
        write_out,
        out_shape=shapes,
        in_specs=[hbm] * 3,
        out_specs=[hbm] * 3,
        scratch_shapes=[pltpu.VMEM(o.shape, o.dtype) for o in shapes] + [pltpu.SemaphoreType.DMA((6,))],
        compiler_params=pltpu.CompilerParams(vmem_limit_bytes=VMEM_LIMIT),
    )(*results)


def solution(mesh):
    n = mesh.shape["parts"]
    in_specs = (
        P(None, None, "parts"),
        P(None, None, "parts"),
        P(),
        P(None, "parts"),
        P(),
        P(None, "parts"),
        P(None, "parts"),
        P("parts"),
        P("parts"),
        P("parts"),
        P("parts"),
    )
    out_specs = (P(None, None, "parts"), P(None, None, "parts"), P(None, "parts"))
    return jax.shard_map(
        functools.partial(body, n, 8), mesh=mesh, in_specs=in_specs, out_specs=out_specs,
        check_vma=False,
    )
```

```python
import functools
import math

import jax
import jax.numpy as jnp
import ml_dtypes
import numpy as np
from jax import lax
from jax.experimental import pallas as pl
from jax.experimental.pallas import tpu as pltpu
from jax.sharding import PartitionSpec as P

SOFT = 0.01
MESH = pl.DeviceIdType.MESH
F32 = jnp.float32
BF16 = jnp.bfloat16
OTHER = 4096
INPUTS = 17
VMEM_LIMIT = 60 * 1024 * 1024
LOAD_ORDER = (9, 3, 7, 8, 0, 1, 11, 5, 6, 15, 2, 4, 10, 12, 13, 14, 16)
LANES = 128
FACE = 16
POINTS = 64


def lobatto_tables():
    points = np.array([-1.0, -math.sqrt(0.2), math.sqrt(0.2), 1.0])
    weights = np.array([1.0, 5.0, 5.0, 1.0]) / 6.0
    derivative = np.zeros((4, 4))
    for a in range(4):
        for b in range(4):
            if a == b:
                derivative[a, b] = sum((1.0 / (points[a] - points[m]) for m in range(4) if m != a))
            else:
                numerator = 1.0
                denominator = 1.0
                for m in range(4):
                    if m != b:
                        denominator *= points[b] - points[m]
                        if m != a:
                            numerator *= points[a] - points[m]
                derivative[a, b] = numerator / denominator
    return (points, weights, derivative)


def shape_gradients():
    points = lobatto_tables()[0]
    gradients = np.zeros((3, 64, 8))
    for q in range(64):
        position = (q // 16, q // 4 % 4, q % 4)
        for k in range(8):
            corner_bits = (k // 4, k // 2 % 2, k % 2)
            for j in range(3):
                factor = 1.0
                for m in range(3):
                    orient = 1.0 if corner_bits[m] == 1 else -1.0
                    if m == j:
                        factor *= 0.5 * orient
                    else:
                        factor *= 0.5 * (1.0 + orient * points[position[m]])
                gradients[j, q, k] = factor
    return gradients


def edge_laplacian():
    matrix = np.zeros((8, 8))
    for k in range(8):
        matrix[k, k] = 3.0
        for b in range(3):
            matrix[k, k ^ 1 << b] = -1.0
    return matrix


def tables():
    _, weights, derivative = lobatto_tables()
    gradients = shape_gradients()
    grid = np.arange(64).reshape(4, 4, 4)
    face_rows = [np.take(grid, 3 * (f % 2), axis=f // 2).reshape(-1) for f in range(6)]
    select = np.zeros((96, 64))
    select[np.arange(96), np.concatenate(face_rows)] = 1.0
    volume = (weights[:, None, None] * weights[None, :, None] * weights[None, None, :]).reshape(-1)
    face_weights = np.tile((weights[:, None] * weights[None, :]).reshape(-1), 6)
    eye = np.eye(4)
    applied = [
        np.kron(derivative, np.kron(eye, eye)),
        np.kron(eye, np.kron(derivative, eye)),
        np.kron(eye, np.kron(eye, derivative)),
    ]
    assembly = np.concatenate(
        [volume[:, None] * m for m in applied] + [select.T * face_weights[None, :]], axis=1
    )
    first = [gradients[(f // 2 + 1) % 3][face_rows[f]] * (2.0 * (f % 2) - 1.0) for f in range(6)]
    second = [gradients[(f // 2 + 2) % 3][face_rows[f]] for f in range(6)]
    tangents = np.concatenate([gradients.reshape(192, 8)] + first + second, axis=0)
    hi, mid, lo = split_table(np.concatenate([tangents, edge_laplacian()], axis=0))
    arrays = (
        np.concatenate([select] * 2, axis=1),
        two_parts(np.concatenate([assembly[:, :192], assembly[:, 224:]], axis=1)),
        two_parts(assembly[:, 192:224]),
        two_parts(assembly.T),
        np.concatenate([hi, hi, hi, mid, mid, lo], axis=1),
        two_parts(tangents.T),
    )
    return [np.ascontiguousarray(a, dtype=np.float32) for a in arrays]


def split_table(a):
    parts, rest = [], a
    for _ in range(3):
        part = rest.astype(ml_dtypes.bfloat16).astype(np.float64)
        parts.append(part)
        rest = rest - part
    return parts


def two_parts(a):
    hi, mid, _ = split_table(a)
    return np.concatenate([hi, mid, hi], axis=1)


def split(x, count):
    parts = []
    for _ in range(count - 1):
        part = x.astype(BF16).astype(F32)
        parts.append(part)
        x = x - part
    return parts + [x]


def rows_of(parts):
    return jnp.concatenate(parts, axis=0).astype(BF16)


def apply_table(table, data):
    hi, lo = split(data, 2)
    return jnp.dot(table, rows_of([hi, hi, lo]), preferred_element_type=F32)


def pick(data, hot, parts=3):
    count = data.shape[0]
    out = jnp.dot(rows_of(split(data, parts)), hot, preferred_element_type=F32)
    return sum(out[k * count:(k + 1) * count] for k in range(parts))


def pick_t(data, hot):
    count = data.shape[0]
    out = lax.dot_general(
        rows_of(split(data, 3)), hot, (((1,), (1,)), ((), ())), preferred_element_type=F32
    )
    return out[:count] + out[count:2 * count] + out[2 * count:]


def cross(a, b):
    return [
        a[1] * b[2] - a[2] * b[1],
        a[2] * b[0] - a[0] * b[2],
        a[0] * b[1] - a[1] * b[0],
    ]


def dot3(a, b):
    return a[0] * b[0] + a[1] * b[1] + a[2] * b[2]


def stacked(a, b):
    if isinstance(a, list):
        return [stacked(x, y) for x, y in zip(a, b)]
    return jnp.concatenate([a, b], axis=0)


class Gas:
    def __init__(self, values):
        self.u, self.m = values, values[1:4]
        self.inv = 1.0 / values[0]
        self.v = [m * self.inv for m in self.m]
        self.p = 0.4 * (values[4] - 0.5 * dot3(self.m, self.v))
        self.h = values[4] + self.p

    def vary(self, tangent):
        self.du, self.dm = tangent, tangent[1:4]
        self.dv = [(self.dm[i] - self.v[i] * tangent[0]) * self.inv for i in range(3)]
        self.dp = 0.4 * (tangent[4] - 0.5 * (dot3(self.dm, self.v) + dot3(self.m, self.dv)))
        self.dh = tangent[4] + self.dp

    @staticmethod
    def merged(a, b):
        both = Gas.__new__(Gas)
        for name, low in vars(a).items():
            setattr(both, name, stacked(low, getattr(b, name)))
        return both

    def along(self, n):
        vn = dot3(self.v, n)
        return [dot3(self.m, n)] + [self.m[k] * vn + self.p * n[k] for k in range(3)] + [self.h * vn]

    def along_change(self, n):
        vn, dvn = dot3(self.v, n), dot3(self.dv, n)
        middle = [self.dm[k] * vn + self.m[k] * dvn + self.dp * n[k] for k in range(3)]
        return [dot3(self.dm, n)] + middle + [self.dh * vn + self.h * dvn]

    def against(self, y):
        common = y[1] * self.m[0] + y[2] * self.m[1] + y[3] * self.m[2] + y[4] * self.h
        return [y[0] * self.m[i] + self.v[i] * common + y[1 + i] * self.p for i in range(3)]

    def speed(self, n, square, size):
        a = dot3(self.v, n)
        root = jnp.sqrt(a * a + SOFT * square)
        self.sound = jnp.sqrt(1.4 * self.p * self.inv)
        inv_root = 1.0 / root
        self.slope = a * inv_root
        sn = SOFT * inv_root + self.sound / size
        return root + self.sound * size, [self.slope * self.v[i] + sn * n[i] for i in range(3)]

    def speed_change(self, n, size):
        dsound = 0.7 * (self.dp - self.p * self.du[0] * self.inv) * self.inv / self.sound
        return self.slope * dot3(self.dv, n) + dsound * size


def kernel(n, group, *refs):
    sources, refs = refs[:INPUTS], refs[INPUTS:]
    results, refs = refs[:3], refs[3:]
    held, refs = refs[:INPUTS], refs[INPUTS:]
    (res_ref, change_ref, update_ref), refs = refs[:3], refs[3:]
    (state_ref, tangent_ref, far_ref, place_ref, damp_ref, neigh_ref, nodes_ref, upper_ref, lower_ref,
     sends_ref, flag_ref, select_ref, asm_ref, asm_halo_ref, asm_t_ref, geo_ref, geo_t_ref) = held
    (up_out, up_in, down_out, down_in, place_out, place_in,
     gup_out, gup_in, gdown_out, gdown_in, sum_out, sum_in, send_sem, recv_sem, load_sem) = refs
    loads = [
        pltpu.make_async_copy(sources[i], held[i], load_sem.at[i]) for i in range(INPUTS)
    ]
    stores = [
        pltpu.make_async_copy(source, results[i], load_sem.at[INPUTS + i])
        for i, source in enumerate((res_ref, change_ref, update_ref))
    ]
    for i in LOAD_ORDER:
        loads[i].start()
    me = lax.axis_index("parts")
    right, left = lax.rem(me + 1, n), lax.rem(me + n - 1, n)
    elements = state_ref.shape[2]
    slots = upper_ref.shape[1]
    owned = place_ref.shape[1]
    shared = sends_ref.shape[1]
    own_pad = -(-owned // LANES) * LANES
    halo_pad = -(-shared // LANES) * LANES
    wide = 2 * elements

    stages = []
    low = 1
    while low < n:
        size = min(group, n // low)
        stages.append([low * k for k in range(1, size)])
        low *= size
    masks = [m for stage in stages for m in stage]

    def partner(mask):
        bit = me // mask % 2 if mask & (mask - 1) == 0 else None
        if bit is not None:
            return me + mask * (1 - 2 * bit)
        result = me
        b = 1
        while b <= mask:
            if mask & b:
                result = result + b * (1 - 2 * (me // b % 2))
            b *= 2
        return result

    partners = [partner(m) for m in masks]

    def remote(index, src, dst, device):
        return pltpu.make_async_remote_copy(
            src_ref=src, dst_ref=dst, send_sem=send_sem.at[index], recv_sem=recv_sem.at[index],
            device_id=(device,), device_id_type=MESH,
        )

    barrier = pltpu.get_barrier_semaphore()
    for device in [left, right] + partners:
        pl.semaphore_signal(barrier, inc=1, device_id=(device,), device_id_type=MESH)

    for i in LOAD_ORDER[:6]:
        loads[i].wait()
    own_rows = lax.broadcasted_iota(jnp.int32, (own_pad, halo_pad), 0)
    sends = sends_ref[...]
    if halo_pad > shared:
        sends = jnp.concatenate([sends, jnp.full((1, halo_pad - shared), -1, jnp.int32)], axis=1)
    sent_nodes = jnp.where(own_rows == sends, 1.0, 0.0).astype(BF16)
    places = jnp.zeros((8, own_pad), F32)
    place = place_ref[...]
    if own_pad > owned:
        place = jnp.concatenate([place, jnp.zeros((3, own_pad - owned), F32)], axis=1)
    places = jnp.concatenate([place, jnp.zeros((5, own_pad), F32)], axis=0)
    place_out[...] = pick(places, sent_nodes)

    row = lax.broadcasted_iota(jnp.int32, (wide, wide), 0)
    in_tangent = row >= elements
    local_key = jnp.where(in_tangent, row - elements + OTHER, row)
    slot = jnp.where(in_tangent, row - elements, row)
    halo_key = jnp.where(slot < slots, local_key + elements, -1)

    def one_hot(key, index):
        return jnp.where(key == index, 1.0, 0.0).astype(BF16)

    def send_hot(index):
        if slots < elements:
            pad = jnp.full((1, elements - slots), -2, jnp.int32)
            index = jnp.concatenate([index, pad, index + OTHER, pad], axis=1)
        else:
            index = jnp.concatenate([index, index + OTHER], axis=1)
        return one_hot(local_key, index)

    values = [state_ref[v] for v in range(5)]
    tangent = [tangent_ref[v] for v in range(5)]
    both = [jnp.concatenate([values[v], tangent[v]], axis=1) for v in range(5)]
    top = POINTS - FACE
    up_out[...] = pick(
        jnp.concatenate([both[v][top:POINTS] for v in range(5)], axis=0), send_hot(upper_ref[...]), 2
    )
    down_out[...] = pick(
        jnp.concatenate([both[v][0:FACE] for v in range(5)], axis=0), send_hot(lower_ref[...]), 2
    )
    pl.semaphore_wait(barrier, 2 + len(partners))
    place_copy = remote(0, place_out, place_in, left)
    up_copy = remote(1, up_out, up_in, right)
    down_copy = remote(2, down_out, down_in, left)
    place_copy.start()
    up_copy.start()
    down_copy.start()

    for i in LOAD_ORDER[6:]:
        loads[i].wait()
    weight = flag_ref[...].astype(F32)
    far_field = far_ref[...]
    damping = damp_ref[...]
    gas = Gas(values)
    select = select_ref[...].astype(BF16)
    traces = jnp.dot(
        select, rows_of(split(jnp.concatenate(both, axis=1), 2)), preferred_element_type=F32
    )
    trace = [traces[:, v * wide:(v + 1) * wide] for v in range(5)]
    neigh = neigh_ref[...]
    neigh = jnp.concatenate([neigh, neigh + OTHER], axis=1)
    far = jnp.where(neigh == elements + slots, 1.0, 0.0).astype(F32)
    outer = []
    for f in range(6):
        opposite = FACE * (f ^ 1)
        stack = jnp.concatenate([trace[v][opposite:opposite + FACE] for v in range(5)], axis=0)
        found = pick(stack, one_hot(local_key, neigh[f:f + 1]), 2)
        outer.append(found)
    nodes = nodes_ref[...]
    nodes = jnp.where(nodes >= owned, nodes + (own_pad - owned), nodes)
    nodes = jnp.concatenate([nodes[k:k + 1] for k in range(8)], axis=1)
    table_rows = lax.broadcasted_iota(jnp.int32, (own_pad + halo_pad, 8 * elements), 0)
    corner_hot = one_hot(table_rows, nodes)

    def corners_of(table):
        found = pick(table, corner_hot)
        return [
            jnp.concatenate(
                [found[i:i + 1, k * elements:(k + 1) * elements] for k in range(8)], axis=0
            )
            for i in range(3)
        ]

    geo = geo_ref[...].astype(BF16)

    def edges_of(corners):
        hi, mid, lo = split(jnp.concatenate(corners, axis=1), 3)
        out = jnp.dot(geo, rows_of([hi, mid, lo, hi, mid, hi]), preferred_element_type=F32)
        rows = [out[:, i * elements:(i + 1) * elements] for i in range(3)]
        volume = [[rows[i][POINTS * j:POINTS * (j + 1)] for i in range(3)] for j in range(3)]
        base = 3 * POINTS
        first = [rows[i][base:base + 6 * FACE] for i in range(3)]
        second = [rows[i][base + 6 * FACE:base + 12 * FACE] for i in range(3)]
        lap = [rows[i][base + 12 * FACE:] for i in range(3)]
        return volume, first, second, lap

    asm = asm_ref[...].astype(BF16)
    asm_halo = asm_halo_ref[...].astype(BF16)
    asm_t = asm_t_ref[...].astype(BF16)
    geo_t = geo_t_ref[...].astype(BF16)

    place_copy.wait()
    corners = corners_of(jnp.concatenate([places, place_in[...]], axis=1))
    edge, first, second, lap = edges_of(corners)
    normals = [cross(edge[(j + 1) % 3], edge[(j + 2) % 3]) for j in range(3)]
    face_n = cross(first, second)
    square = dot3(face_n, face_n)
    size = jnp.sqrt(square)

    flux = [gas.along(normals[j]) for j in range(3)]
    split_row = 2 * FACE

    def faces(begin, end):
        rows = slice(FACE * begin, FACE * end)
        side = [
            jnp.concatenate(
                [
                    outer[f][FACE * v:FACE * (v + 1)] + far[f:f + 1] * far_field[:, v:v + 1]
                    for f in range(begin, end)
                ],
                axis=0,
            )
            for v in range(5)
        ]
        normal, area, extent = [x[rows] for x in face_n], square[rows], size[rows]
        inner = Gas([t[rows, :elements] for t in trace])
        other = Gas([t[:, :elements] for t in side])
        inner_speed, inner_grad = inner.speed(normal, area, extent)
        other_speed, other_grad = other.speed(normal, area, extent)
        gap = inner_speed - other_speed
        root = jnp.sqrt(gap * gap + SOFT * area)
        inv_root = 0.5 / root
        lam = 0.5 * (inner_speed + other_speed) + 0.5 * root
        lam_n = [
            0.5 * (inner_grad[i] + other_grad[i])
            + (gap * (inner_grad[i] - other_grad[i]) + SOFT * normal[i]) * inv_root
            for i in range(3)
        ]
        diff = [other.u[v] - inner.u[v] for v in range(5)]
        one, two = inner.along(normal), other.along(normal)
        jump = [0.5 * (two[v] - one[v] - lam * diff[v]) for v in range(5)]
        return inner, other, jump, [side, gap, inv_root, lam, lam_n, diff]

    def local_part(fluxes, jump):
        data = [
            jnp.concatenate([fluxes[0][v], fluxes[1][v], fluxes[2][v], jump[v]], axis=0)
            for v in range(5)
        ]
        return apply_table(asm, jnp.concatenate(data, axis=1))

    def halo_part_of(jump):
        return apply_table(asm_halo, jnp.concatenate(jump, axis=1))

    def assembled(fluxes, jump):
        first_rows = [x[:split_row] for x in jump]
        return local_part(fluxes, [x[split_row:] for x in jump]) + halo_part_of(first_rows)

    inner_b, other_b, jump, fields_b = faces(2, 6)
    result = local_part(flux, jump)

    up_hot, down_hot = one_hot(halo_key, neigh[0:1]), one_hot(halo_key, neigh[1:2])
    up_copy.wait()
    outer[0] = outer[0] + pick(up_in[...], up_hot, 2)
    down_copy.wait()
    outer[1] = outer[1] + pick(down_in[...], down_hot, 2)
    inner_a, other_a, jump, fields_a = faces(0, 2)
    result = result + halo_part_of(jump)
    inner, other = Gas.merged(inner_a, inner_b), Gas.merged(other_a, other_b)
    side, gap, inv_root, lam, lam_n, diff = stacked(fields_a, fields_b)
    weighted = []
    for v in range(5):
        residual = result[:, v * elements:(v + 1) * elements]
        res_ref[v] = residual
        weighted.append(residual * weight)
    stores[0].start()

    back = [apply_table(asm_t, weighted[v]) for v in range(5)]
    grads = [gas.against([b[POINTS * j:POINTS * (j + 1)] for b in back]) for j in range(3)]
    face_back = [b[3 * POINTS:] for b in back]
    across = sum(face_back[v] * diff[v] for v in range(5))
    inner_against, other_against = inner.against(face_back), other.against(face_back)
    face_grad = [
        0.5 * (other_against[i] - inner_against[i] - across * lam_n[i]) for i in range(3)
    ]
    edge_grad = []
    for j in range(3):
        one = cross(edge[(j + 1) % 3], grads[(j + 2) % 3])
        two = cross(grads[(j + 1) % 3], edge[(j + 2) % 3])
        edge_grad.append([one[i] + two[i] for i in range(3)])
    first_grad, second_grad = cross(second, face_grad), cross(face_grad, first)
    smoothing = damping[:, 1:2]
    stack = [
        jnp.concatenate(
            [edge_grad[0][i], edge_grad[1][i], edge_grad[2][i], first_grad[i], second_grad[i]], axis=0
        )
        for i in range(3)
    ]
    pulled = apply_table(geo_t, jnp.concatenate(stack, axis=1))
    rows = []
    for i in range(3):
        corner_grad = pulled[:, i * elements:(i + 1) * elements] + smoothing * weight * lap[i]
        rows.append(jnp.concatenate([corner_grad[k:k + 1] for k in range(8)], axis=1))
    rows.append(jnp.concatenate([weight] * 8, axis=1))
    rows.append(jnp.zeros((4, 8 * elements), F32))
    table = pick_t(jnp.concatenate(rows, axis=0), corner_hot)
    own_part, halo_part = table[:, :own_pad], table[:, own_pad:]

    gup_out[...] = halo_part
    gup_copy = remote(3, gup_out, gup_in, right)
    gup_copy.start()
    gdown_out[...] = pick(own_part, sent_nodes)
    gdown_copy = remote(4, gdown_out, gdown_in, left)
    gdown_copy.start()

    gas.vary(tangent)
    inner.vary([t[:, elements:] for t in trace])
    other.vary([t[:, elements:] for t in side])
    flux_change = [gas.along_change(normals[j]) for j in range(3)]
    inner_dspeed, other_dspeed = inner.speed_change(face_n, size), other.speed_change(face_n, size)
    dlam = 0.5 * (inner_dspeed + other_dspeed) + gap * (inner_dspeed - other_dspeed) * inv_root
    inner_change, other_change = inner.along_change(face_n), other.along_change(face_n)
    jump = []
    for v in range(5):
        ddiff = other.du[v] - inner.du[v]
        jump.append(0.5 * (other_change[v] - inner_change[v] - dlam * diff[v] - lam * ddiff))
    result = assembled(flux_change, jump)
    for v in range(5):
        change_ref[v] = result[:, v * elements:(v + 1) * elements]
    stores[1].start()

    def descent_of(total):
        line = lax.broadcasted_iota(jnp.int32, total.shape, 0)
        touched = jnp.where(total[3:4] > 0.5, 1.0, 0.0)
        return -jnp.where(line < 3, total * touched, 0.0)

    gup_copy.wait()
    descent = descent_of(own_part + pick_t(gup_in[...], sent_nodes))
    gdown_copy.wait()
    halo_descent = descent_of(halo_part + gdown_in[...])

    steps = corners_of(jnp.concatenate([descent, halo_descent], axis=1))
    dedge, dfirst, dsecond, dlap = edges_of(steps)
    dflux = []
    for j in range(3):
        a, b = (j + 1) % 3, (j + 2) % 3
        one, two = cross(dedge[a], edge[b]), cross(edge[a], dedge[b])
        dflux.append(gas.along([one[i] + two[i] for i in range(3)]))
    one, two = cross(dfirst, second), cross(first, dsecond)
    dface = [one[i] + two[i] for i in range(3)]
    inner_dalong, other_dalong = inner.along(dface), other.along(dface)
    dlam_n = dot3(lam_n, dface)
    jump = [
        0.5 * (other_dalong[v] - inner_dalong[v] - dlam_n * diff[v]) for v in range(5)
    ]
    moved = assembled(dflux, jump)
    squares = jnp.sum(moved * moved, axis=0, keepdims=True)
    squares = sum(squares[:, v * elements:(v + 1) * elements] for v in range(5))
    curvature = squares * weight
    bent = sum(steps[i] * dlap[i] for i in range(3))
    bending = smoothing * jnp.sum(bent, axis=0, keepdims=True) * weight
    norm = jnp.sum(descent * descent, axis=0, keepdims=True)
    both_sums = jnp.sum(curvature + bending, axis=1, keepdims=True)
    norm_sum = jnp.sum(norm, axis=1, keepdims=True)
    line = lax.broadcasted_iota(jnp.int32, (8, LANES), 0)
    sums = jnp.where(line == 0, norm_sum, jnp.where(line == 1, both_sums, 0.0))

    index = 0
    for s, stage in enumerate(stages):
        sum_out[s] = sums
        copies = []
        for _ in stage:
            copies.append(remote(5 + index, sum_out.at[s], sum_in.at[index], partners[index]))
            copies[-1].start()
            index += 1
        for i, copy in enumerate(copies):
            copy.wait_recv()
        for i in range(len(stage)):
            sums = sums + sum_in[index - len(stage) + i]
        for copy in copies:
            copy.wait_send()
    norm_total, rest = sums[0:1, 0:1], sums[1:2, 0:1]
    step_size = norm_total / (rest + damping[:, 0:1] * norm_total)
    update_ref[...] = (descent * step_size)[0:3, :owned]
    stores[2].start()
    for store in stores:
        store.wait()


def write_out(*refs):
    loads = [pltpu.make_async_copy(refs[i], refs[6 + i], refs[9].at[i]) for i in range(3)]
    stores = [pltpu.make_async_copy(refs[6 + i], refs[3 + i], refs[9].at[3 + i]) for i in range(3)]
    for load in loads:
        load.start()
    for load, store in zip(loads, stores):
        load.wait()
        store.start()
    for store in stores:
        store.wait()


def body(n, group, flow_state, state_tangent, far_field, coordinates, damping, face_neighbour,
         element_nodes, upper_sends, lower_sends, node_sends, shock_flags):
    own_pad = -(-coordinates.shape[1] // LANES) * LANES
    halo_pad = -(-node_sends.shape[0] // LANES) * LANES
    wide = 2 * flow_state.shape[2]
    count, stages, low = 0, 0, 1
    while low < n:
        size = min(group, n // low)
        count, stages, low = count + size - 1, stages + 1, low * size
    hbm = pl.BlockSpec(memory_space=pltpu.HBM)
    constants = [jnp.asarray(t) for t in tables()]
    halo = pltpu.VMEM((5 * FACE, wide), F32)
    place = pltpu.VMEM((8, halo_pad), F32)
    operands = [
        flow_state, state_tangent, far_field.reshape(1, -1), coordinates, damping.reshape(1, -1),
        face_neighbour, element_nodes,
        upper_sends.reshape(1, -1), lower_sends.reshape(1, -1), node_sends.reshape(1, -1),
        shock_flags.reshape(1, -1),
    ] + constants
    shapes = (
        jax.ShapeDtypeStruct(flow_state.shape, F32),
        jax.ShapeDtypeStruct(flow_state.shape, F32),
        jax.ShapeDtypeStruct(coordinates.shape, F32),
    )
    results = pl.pallas_call(
        functools.partial(kernel, n, group),
        out_shape=shapes,
        in_specs=[hbm] * len(operands),
        out_specs=(hbm, hbm, hbm),
        scratch_shapes=[pltpu.VMEM(o.shape, o.dtype) for o in operands + list(shapes)] + [halo] * 4 + [place] * 6 + [
            pltpu.VMEM((stages, 8, LANES), F32),
            pltpu.VMEM((count, 8, LANES), F32),
            pltpu.SemaphoreType.DMA((5 + count,)),
            pltpu.SemaphoreType.DMA((5 + count,)),
            pltpu.SemaphoreType.DMA((INPUTS + 3,)),
        ],
        compiler_params=pltpu.CompilerParams(
            collective_id=0, has_side_effects=True, vmem_limit_bytes=VMEM_LIMIT
        ),
    )(*operands)
    return pl.pallas_call(
        write_out,
        out_shape=shapes,
        in_specs=[hbm] * 3,
        out_specs=[hbm] * 3,
        scratch_shapes=[pltpu.VMEM(o.shape, o.dtype) for o in shapes] + [pltpu.SemaphoreType.DMA((6,))],
        compiler_params=pltpu.CompilerParams(vmem_limit_bytes=VMEM_LIMIT),
    )(*results)


def solution(mesh):
    n = mesh.shape["parts"]
    in_specs = (
        P(None, None, "parts"),
        P(None, None, "parts"),
        P(),
        P(None, "parts"),
        P(),
        P(None, "parts"),
        P(None, "parts"),
        P("parts"),
        P("parts"),
        P("parts"),
        P("parts"),
    )
    out_specs = (P(None, None, "parts"), P(None, None, "parts"), P(None, "parts"))
    return jax.shard_map(
        functools.partial(body, n, 8), mesh=mesh, in_specs=in_specs, out_specs=out_specs,
        check_vma=False,
    )
```

```python
import functools
import math

import jax
import jax.numpy as jnp
import ml_dtypes
import numpy as np
from jax import lax
from jax.experimental import pallas as pl
from jax.experimental.pallas import tpu as pltpu
from jax.sharding import PartitionSpec as P

SOFT = 0.01
MESH = pl.DeviceIdType.MESH
F32 = jnp.float32
BF16 = jnp.bfloat16
OTHER = 4096
INPUTS = 17
VMEM_LIMIT = 60 * 1024 * 1024
LOAD_ORDER = (9, 3, 7, 8, 0, 1, 11, 5, 6, 15, 2, 4, 10, 12, 13, 14, 16)
LANES = 128
FACE = 16
POINTS = 64


def lobatto_tables():
    points = np.array([-1.0, -math.sqrt(0.2), math.sqrt(0.2), 1.0])
    weights = np.array([1.0, 5.0, 5.0, 1.0]) / 6.0
    derivative = np.zeros((4, 4))
    for a in range(4):
        for b in range(4):
            if a == b:
                derivative[a, b] = sum((1.0 / (points[a] - points[m]) for m in range(4) if m != a))
            else:
                numerator = 1.0
                denominator = 1.0
                for m in range(4):
                    if m != b:
                        denominator *= points[b] - points[m]
                        if m != a:
                            numerator *= points[a] - points[m]
                derivative[a, b] = numerator / denominator
    return (points, weights, derivative)


def shape_gradients():
    points = lobatto_tables()[0]
    gradients = np.zeros((3, 64, 8))
    for q in range(64):
        position = (q // 16, q // 4 % 4, q % 4)
        for k in range(8):
            corner_bits = (k // 4, k // 2 % 2, k % 2)
            for j in range(3):
                factor = 1.0
                for m in range(3):
                    orient = 1.0 if corner_bits[m] == 1 else -1.0
                    if m == j:
                        factor *= 0.5 * orient
                    else:
                        factor *= 0.5 * (1.0 + orient * points[position[m]])
                gradients[j, q, k] = factor
    return gradients


def edge_laplacian():
    matrix = np.zeros((8, 8))
    for k in range(8):
        matrix[k, k] = 3.0
        for b in range(3):
            matrix[k, k ^ 1 << b] = -1.0
    return matrix


def tables():
    _, weights, derivative = lobatto_tables()
    gradients = shape_gradients()
    grid = np.arange(64).reshape(4, 4, 4)
    face_rows = [np.take(grid, 3 * (f % 2), axis=f // 2).reshape(-1) for f in range(6)]
    select = np.zeros((96, 64))
    select[np.arange(96), np.concatenate(face_rows)] = 1.0
    volume = (weights[:, None, None] * weights[None, :, None] * weights[None, None, :]).reshape(-1)
    face_weights = np.tile((weights[:, None] * weights[None, :]).reshape(-1), 6)
    eye = np.eye(4)
    applied = [
        np.kron(derivative, np.kron(eye, eye)),
        np.kron(eye, np.kron(derivative, eye)),
        np.kron(eye, np.kron(eye, derivative)),
    ]
    assembly = np.concatenate(
        [volume[:, None] * m for m in applied] + [select.T * face_weights[None, :]], axis=1
    )
    first = [gradients[(f // 2 + 1) % 3][face_rows[f]] * (2.0 * (f % 2) - 1.0) for f in range(6)]
    second = [gradients[(f // 2 + 2) % 3][face_rows[f]] for f in range(6)]
    tangents = np.concatenate([gradients.reshape(192, 8)] + first + second, axis=0)
    hi, mid, lo = split_table(np.concatenate([tangents, edge_laplacian()], axis=0))
    arrays = (
        np.concatenate([select] * 2, axis=1),
        two_parts(np.concatenate([assembly[:, :192], assembly[:, 224:]], axis=1)),
        two_parts(assembly[:, 192:224]),
        two_parts(assembly.T),
        np.concatenate([hi, hi, hi, mid, mid, lo], axis=1),
        two_parts(tangents.T),
    )
    return [np.ascontiguousarray(a, dtype=np.float32) for a in arrays]


def split_table(a):
    parts, rest = [], a
    for _ in range(3):
        part = rest.astype(ml_dtypes.bfloat16).astype(np.float64)
        parts.append(part)
        rest = rest - part
    return parts


def two_parts(a):
    hi, mid, _ = split_table(a)
    return np.concatenate([hi, mid, hi], axis=1)


def split(x, count):
    parts = []
    for _ in range(count - 1):
        part = x.astype(BF16).astype(F32)
        parts.append(part)
        x = x - part
    return parts + [x]


def rows_of(parts):
    return jnp.concatenate(parts, axis=0).astype(BF16)


def apply_table(table, data):
    hi, lo = split(data, 2)
    return jnp.dot(table, rows_of([hi, hi, lo]), preferred_element_type=F32)


def pick(data, hot, parts=3):
    count = data.shape[0]
    out = jnp.dot(rows_of(split(data, parts)), hot, preferred_element_type=F32)
    return sum(out[k * count:(k + 1) * count] for k in range(parts))


def pick_t(data, hot):
    count = data.shape[0]
    out = lax.dot_general(
        rows_of(split(data, 3)), hot, (((1,), (1,)), ((), ())), preferred_element_type=F32
    )
    return out[:count] + out[count:2 * count] + out[2 * count:]


def cross(a, b):
    return [
        a[1] * b[2] - a[2] * b[1],
        a[2] * b[0] - a[0] * b[2],
        a[0] * b[1] - a[1] * b[0],
    ]


def dot3(a, b):
    return a[0] * b[0] + a[1] * b[1] + a[2] * b[2]


def stacked(a, b):
    if isinstance(a, list):
        return [stacked(x, y) for x, y in zip(a, b)]
    return jnp.concatenate([a, b], axis=0)


class Gas:
    def __init__(self, values):
        self.u, self.m = values, values[1:4]
        self.inv = 1.0 / values[0]
        self.v = [m * self.inv for m in self.m]
        self.p = 0.4 * (values[4] - 0.5 * dot3(self.m, self.v))
        self.h = values[4] + self.p

    def vary(self, tangent):
        self.du, self.dm = tangent, tangent[1:4]
        self.dv = [(self.dm[i] - self.v[i] * tangent[0]) * self.inv for i in range(3)]
        self.dp = 0.4 * (tangent[4] - 0.5 * (dot3(self.dm, self.v) + dot3(self.m, self.dv)))
        self.dh = tangent[4] + self.dp

    @staticmethod
    def merged(a, b):
        both = Gas.__new__(Gas)
        for name, low in vars(a).items():
            setattr(both, name, stacked(low, getattr(b, name)))
        return both

    def along(self, n):
        vn = dot3(self.v, n)
        return [dot3(self.m, n)] + [self.m[k] * vn + self.p * n[k] for k in range(3)] + [self.h * vn]

    def along_change(self, n):
        vn, dvn = dot3(self.v, n), dot3(self.dv, n)
        middle = [self.dm[k] * vn + self.m[k] * dvn + self.dp * n[k] for k in range(3)]
        return [dot3(self.dm, n)] + middle + [self.dh * vn + self.h * dvn]

    def against(self, y):
        common = y[1] * self.m[0] + y[2] * self.m[1] + y[3] * self.m[2] + y[4] * self.h
        return [y[0] * self.m[i] + self.v[i] * common + y[1 + i] * self.p for i in range(3)]

    def speed(self, n, square, size):
        a = dot3(self.v, n)
        root = jnp.sqrt(a * a + SOFT * square)
        self.sound = jnp.sqrt(1.4 * self.p * self.inv)
        inv_root = 1.0 / root
        self.slope = a * inv_root
        sn = SOFT * inv_root + self.sound / size
        return root + self.sound * size, [self.slope * self.v[i] + sn * n[i] for i in range(3)]

    def speed_change(self, n, size):
        dsound = 0.7 * (self.dp - self.p * self.du[0] * self.inv) * self.inv / self.sound
        return self.slope * dot3(self.dv, n) + dsound * size


def kernel(n, group, *refs):
    sources, refs = refs[:INPUTS], refs[INPUTS:]
    results, refs = refs[:3], refs[3:]
    held, refs = refs[:INPUTS], refs[INPUTS:]
    (res_ref, change_ref, update_ref), refs = refs[:3], refs[3:]
    (state_ref, tangent_ref, far_ref, place_ref, damp_ref, neigh_ref, nodes_ref, upper_ref, lower_ref,
     sends_ref, flag_ref, select_ref, asm_ref, asm_halo_ref, asm_t_ref, geo_ref, geo_t_ref) = held
    (up_out, up_in, down_out, down_in, place_out, place_in,
     gup_out, gup_in, gdown_out, gdown_in, sum_out, sum_in, send_sem, recv_sem, load_sem) = refs
    loads = [
        pltpu.make_async_copy(sources[i], held[i], load_sem.at[i]) for i in range(INPUTS)
    ]
    stores = [
        pltpu.make_async_copy(source, results[i], load_sem.at[INPUTS + i])
        for i, source in enumerate((res_ref, change_ref, update_ref))
    ]
    for i in LOAD_ORDER[:6]:
        loads[i].start()
    me = lax.axis_index("parts")
    right, left = lax.rem(me + 1, n), lax.rem(me + n - 1, n)
    elements = state_ref.shape[2]
    slots = upper_ref.shape[1]
    owned = place_ref.shape[1]
    shared = sends_ref.shape[1]
    own_pad = -(-owned // LANES) * LANES
    halo_pad = -(-shared // LANES) * LANES
    wide = 2 * elements

    stages = []
    low = 1
    while low < n:
        size = min(group, n // low)
        stages.append([low * k for k in range(1, size)])
        low *= size
    masks = [m for stage in stages for m in stage]

    def partner(mask):
        bit = me // mask % 2 if mask & (mask - 1) == 0 else None
        if bit is not None:
            return me + mask * (1 - 2 * bit)
        result = me
        b = 1
        while b <= mask:
            if mask & b:
                result = result + b * (1 - 2 * (me // b % 2))
            b *= 2
        return result

    partners = [partner(m) for m in masks]

    def remote(index, src, dst, device):
        return pltpu.make_async_remote_copy(
            src_ref=src, dst_ref=dst, send_sem=send_sem.at[index], recv_sem=recv_sem.at[index],
            device_id=(device,), device_id_type=MESH,
        )

    barrier = pltpu.get_barrier_semaphore()
    for device in [left, right] + partners:
        pl.semaphore_signal(barrier, inc=1, device_id=(device,), device_id_type=MESH)

    for i in LOAD_ORDER[6:]:
        loads[i].start()

    for i in LOAD_ORDER[:6]:
        loads[i].wait()
    own_rows = lax.broadcasted_iota(jnp.int32, (own_pad, halo_pad), 0)
    sends = sends_ref[...]
    if halo_pad > shared:
        sends = jnp.concatenate([sends, jnp.full((1, halo_pad - shared), -1, jnp.int32)], axis=1)
    sent_nodes = jnp.where(own_rows == sends, 1.0, 0.0).astype(BF16)
    places = jnp.zeros((8, own_pad), F32)
    place = place_ref[...]
    if own_pad > owned:
        place = jnp.concatenate([place, jnp.zeros((3, own_pad - owned), F32)], axis=1)
    places = jnp.concatenate([place, jnp.zeros((5, own_pad), F32)], axis=0)
    place_out[...] = pick(places, sent_nodes)

    row = lax.broadcasted_iota(jnp.int32, (wide, wide), 0)
    in_tangent = row >= elements
    local_key = jnp.where(in_tangent, row - elements + OTHER, row)
    slot = jnp.where(in_tangent, row - elements, row)
    halo_key = jnp.where(slot < slots, local_key + elements, -1)

    def one_hot(key, index):
        return jnp.where(key == index, 1.0, 0.0).astype(BF16)

    def send_hot(index):
        if slots < elements:
            pad = jnp.full((1, elements - slots), -2, jnp.int32)
            index = jnp.concatenate([index, pad, index + OTHER, pad], axis=1)
        else:
            index = jnp.concatenate([index, index + OTHER], axis=1)
        return one_hot(local_key, index)

    values = [state_ref[v] for v in range(5)]
    tangent = [tangent_ref[v] for v in range(5)]
    both = [jnp.concatenate([values[v], tangent[v]], axis=1) for v in range(5)]
    top = POINTS - FACE
    up_out[...] = pick(
        jnp.concatenate([both[v][top:POINTS] for v in range(5)], axis=0), send_hot(upper_ref[...]), 2
    )
    down_out[...] = pick(
        jnp.concatenate([both[v][0:FACE] for v in range(5)], axis=0), send_hot(lower_ref[...]), 2
    )
    pl.semaphore_wait(barrier, 2 + len(partners))
    place_copy = remote(0, place_out, place_in, left)
    up_copy = remote(1, up_out, up_in, right)
    down_copy = remote(2, down_out, down_in, left)
    place_copy.start()
    up_copy.start()
    down_copy.start()

    for i in LOAD_ORDER[6:]:
        loads[i].wait()
    weight = flag_ref[...].astype(F32)
    far_field = far_ref[...]
    damping = damp_ref[...]
    gas = Gas(values)
    select = select_ref[...].astype(BF16)
    traces = jnp.dot(
        select, rows_of(split(jnp.concatenate(both, axis=1), 2)), preferred_element_type=F32
    )
    trace = [traces[:, v * wide:(v + 1) * wide] for v in range(5)]
    neigh = neigh_ref[...]
    neigh = jnp.concatenate([neigh, neigh + OTHER], axis=1)
    far = jnp.where(neigh == elements + slots, 1.0, 0.0).astype(F32)
    outer = []
    for f in range(6):
        opposite = FACE * (f ^ 1)
        stack = jnp.concatenate([trace[v][opposite:opposite + FACE] for v in range(5)], axis=0)
        found = pick(stack, one_hot(local_key, neigh[f:f + 1]), 2)
        outer.append(found)
    nodes = nodes_ref[...]
    nodes = jnp.where(nodes >= owned, nodes + (own_pad - owned), nodes)
    nodes = jnp.concatenate([nodes[k:k + 1] for k in range(8)], axis=1)
    table_rows = lax.broadcasted_iota(jnp.int32, (own_pad + halo_pad, 8 * elements), 0)
    corner_hot = one_hot(table_rows, nodes)

    def corners_of(table):
        found = pick(table, corner_hot)
        return [
            jnp.concatenate(
                [found[i:i + 1, k * elements:(k + 1) * elements] for k in range(8)], axis=0
            )
            for i in range(3)
        ]

    geo = geo_ref[...].astype(BF16)

    def edges_of(corners):
        rows = []
        for corner in corners:
            hi, mid, lo = split(corner, 3)
            data = rows_of([hi, mid, lo, hi, mid, hi])
            rows.append(jnp.dot(geo, data, preferred_element_type=F32))
        volume = [[rows[i][POINTS * j:POINTS * (j + 1)] for i in range(3)] for j in range(3)]
        base = 3 * POINTS
        first = [rows[i][base:base + 6 * FACE] for i in range(3)]
        second = [rows[i][base + 6 * FACE:base + 12 * FACE] for i in range(3)]
        lap = [rows[i][base + 12 * FACE:] for i in range(3)]
        return volume, first, second, lap

    asm = asm_ref[...].astype(BF16)
    asm_halo = asm_halo_ref[...].astype(BF16)
    asm_t = asm_t_ref[...].astype(BF16)
    geo_t = geo_t_ref[...].astype(BF16)

    place_copy.wait()
    corners = corners_of(jnp.concatenate([places, place_in[...]], axis=1))
    edge, first, second, lap = edges_of(corners)
    normals = [cross(edge[(j + 1) % 3], edge[(j + 2) % 3]) for j in range(3)]
    face_n = cross(first, second)
    square = dot3(face_n, face_n)
    size = jnp.sqrt(square)

    flux = [gas.along(normals[j]) for j in range(3)]
    split_row = 2 * FACE

    def faces(begin, end):
        rows = slice(FACE * begin, FACE * end)
        side = [
            jnp.concatenate(
                [
                    outer[f][FACE * v:FACE * (v + 1)] + far[f:f + 1] * far_field[:, v:v + 1]
                    for f in range(begin, end)
                ],
                axis=0,
            )
            for v in range(5)
        ]
        normal, area, extent = [x[rows] for x in face_n], square[rows], size[rows]
        inner = Gas([t[rows, :elements] for t in trace])
        other = Gas([t[:, :elements] for t in side])
        inner_speed, inner_grad = inner.speed(normal, area, extent)
        other_speed, other_grad = other.speed(normal, area, extent)
        gap = inner_speed - other_speed
        root = jnp.sqrt(gap * gap + SOFT * area)
        inv_root = 0.5 / root
        lam = 0.5 * (inner_speed + other_speed) + 0.5 * root
        lam_n = [
            0.5 * (inner_grad[i] + other_grad[i])
            + (gap * (inner_grad[i] - other_grad[i]) + SOFT * normal[i]) * inv_root
            for i in range(3)
        ]
        diff = [other.u[v] - inner.u[v] for v in range(5)]
        one, two = inner.along(normal), other.along(normal)
        jump = [0.5 * (two[v] - one[v] - lam * diff[v]) for v in range(5)]
        return inner, other, jump, [side, gap, inv_root, lam, lam_n, diff]

    def local_part(fluxes, jump):
        data = [
            jnp.concatenate([fluxes[0][v], fluxes[1][v], fluxes[2][v], jump[v]], axis=0)
            for v in range(5)
        ]
        return apply_table(asm, jnp.concatenate(data, axis=1))

    def halo_part_of(jump):
        return apply_table(asm_halo, jnp.concatenate(jump, axis=1))

    def assembled(fluxes, jump):
        first_rows = [x[:split_row] for x in jump]
        return local_part(fluxes, [x[split_row:] for x in jump]) + halo_part_of(first_rows)

    inner_b, other_b, jump, fields_b = faces(2, 6)
    result = local_part(flux, jump)

    up_hot, down_hot = one_hot(halo_key, neigh[0:1]), one_hot(halo_key, neigh[1:2])
    up_copy.wait()
    outer[0] = outer[0] + pick(up_in[...], up_hot, 2)
    down_copy.wait()
    outer[1] = outer[1] + pick(down_in[...], down_hot, 2)
    inner_a, other_a, jump, fields_a = faces(0, 2)
    result = result + halo_part_of(jump)
    inner, other = Gas.merged(inner_a, inner_b), Gas.merged(other_a, other_b)
    side, gap, inv_root, lam, lam_n, diff = stacked(fields_a, fields_b)
    weighted = []
    for v in range(5):
        residual = result[:, v * elements:(v + 1) * elements]
        res_ref[v] = residual
        weighted.append(residual * weight)
    stores[0].start()

    back = [apply_table(asm_t, weighted[v]) for v in range(5)]
    grads = [gas.against([b[POINTS * j:POINTS * (j + 1)] for b in back]) for j in range(3)]
    face_back = [b[3 * POINTS:] for b in back]
    across = sum(face_back[v] * diff[v] for v in range(5))
    inner_against, other_against = inner.against(face_back), other.against(face_back)
    face_grad = [
        0.5 * (other_against[i] - inner_against[i] - across * lam_n[i]) for i in range(3)
    ]
    edge_grad = []
    for j in range(3):
        one = cross(edge[(j + 1) % 3], grads[(j + 2) % 3])
        two = cross(grads[(j + 1) % 3], edge[(j + 2) % 3])
        edge_grad.append([one[i] + two[i] for i in range(3)])
    first_grad, second_grad = cross(second, face_grad), cross(face_grad, first)
    smoothing = damping[:, 1:2]
    stack = [
        jnp.concatenate(
            [edge_grad[0][i], edge_grad[1][i], edge_grad[2][i], first_grad[i], second_grad[i]], axis=0
        )
        for i in range(3)
    ]
    pulled = apply_table(geo_t, jnp.concatenate(stack, axis=1))
    rows = []
    for i in range(3):
        corner_grad = pulled[:, i * elements:(i + 1) * elements] + smoothing * weight * lap[i]
        rows.append(jnp.concatenate([corner_grad[k:k + 1] for k in range(8)], axis=1))
    rows.append(jnp.concatenate([weight] * 8, axis=1))
    rows.append(jnp.zeros((4, 8 * elements), F32))
    table = pick_t(jnp.concatenate(rows, axis=0), corner_hot)
    own_part, halo_part = table[:, :own_pad], table[:, own_pad:]

    gup_out[...] = halo_part
    gup_copy = remote(3, gup_out, gup_in, right)
    gup_copy.start()
    gdown_out[...] = pick(own_part, sent_nodes)
    gdown_copy = remote(4, gdown_out, gdown_in, left)
    gdown_copy.start()

    gas.vary(tangent)
    inner.vary([t[:, elements:] for t in trace])
    other.vary([t[:, elements:] for t in side])
    flux_change = [gas.along_change(normals[j]) for j in range(3)]
    inner_dspeed, other_dspeed = inner.speed_change(face_n, size), other.speed_change(face_n, size)
    dlam = 0.5 * (inner_dspeed + other_dspeed) + gap * (inner_dspeed - other_dspeed) * inv_root
    inner_change, other_change = inner.along_change(face_n), other.along_change(face_n)
    jump = []
    for v in range(5):
        ddiff = other.du[v] - inner.du[v]
        jump.append(0.5 * (other_change[v] - inner_change[v] - dlam * diff[v] - lam * ddiff))
    result = assembled(flux_change, jump)
    for v in range(5):
        change_ref[v] = result[:, v * elements:(v + 1) * elements]
    stores[1].start()

    def descent_of(total):
        line = lax.broadcasted_iota(jnp.int32, total.shape, 0)
        touched = jnp.where(total[3:4] > 0.5, 1.0, 0.0)
        return -jnp.where(line < 3, total * touched, 0.0)

    gup_copy.wait()
    descent = descent_of(own_part + pick_t(gup_in[...], sent_nodes))
    gdown_copy.wait()
    halo_descent = descent_of(halo_part + gdown_in[...])

    steps = corners_of(jnp.concatenate([descent, halo_descent], axis=1))
    dedge, dfirst, dsecond, dlap = edges_of(steps)
    dflux = []
    for j in range(3):
        a, b = (j + 1) % 3, (j + 2) % 3
        one, two = cross(dedge[a], edge[b]), cross(edge[a], dedge[b])
        dflux.append(gas.along([one[i] + two[i] for i in range(3)]))
    one, two = cross(dfirst, second), cross(first, dsecond)
    dface = [one[i] + two[i] for i in range(3)]
    inner_dalong, other_dalong = inner.along(dface), other.along(dface)
    dlam_n = dot3(lam_n, dface)
    jump = [
        0.5 * (other_dalong[v] - inner_dalong[v] - dlam_n * diff[v]) for v in range(5)
    ]
    moved = assembled(dflux, jump)
    squares = jnp.sum(moved * moved, axis=0, keepdims=True)
    squares = sum(squares[:, v * elements:(v + 1) * elements] for v in range(5))
    curvature = squares * weight
    bent = sum(steps[i] * dlap[i] for i in range(3))
    bending = smoothing * jnp.sum(bent, axis=0, keepdims=True) * weight
    norm = jnp.sum(descent * descent, axis=0, keepdims=True)
    both_sums = jnp.sum(curvature + bending, axis=1, keepdims=True)
    norm_sum = jnp.sum(norm, axis=1, keepdims=True)
    line = lax.broadcasted_iota(jnp.int32, (8, LANES), 0)
    sums = jnp.where(line == 0, norm_sum, jnp.where(line == 1, both_sums, 0.0))

    index = 0
    for s, stage in enumerate(stages):
        sum_out[s] = sums
        copies = []
        for _ in stage:
            copies.append(remote(5 + index, sum_out.at[s], sum_in.at[index], partners[index]))
            copies[-1].start()
            index += 1
        for i, copy in enumerate(copies):
            copy.wait_recv()
        for i in range(len(stage)):
            sums = sums + sum_in[index - len(stage) + i]
        for copy in copies:
            copy.wait_send()
    norm_total, rest = sums[0:1, 0:1], sums[1:2, 0:1]
    step_size = norm_total / (rest + damping[:, 0:1] * norm_total)
    update_ref[...] = (descent * step_size)[0:3, :owned]
    stores[2].start()
    for store in stores:
        store.wait()


def write_out(*refs):
    loads = [pltpu.make_async_copy(refs[i], refs[6 + i], refs[9].at[i]) for i in range(3)]
    stores = [pltpu.make_async_copy(refs[6 + i], refs[3 + i], refs[9].at[3 + i]) for i in range(3)]
    for load in loads:
        load.start()
    for load, store in zip(loads, stores):
        load.wait()
        store.start()
    for store in stores:
        store.wait()


def body(n, group, flow_state, state_tangent, far_field, coordinates, damping, face_neighbour,
         element_nodes, upper_sends, lower_sends, node_sends, shock_flags):
    own_pad = -(-coordinates.shape[1] // LANES) * LANES
    halo_pad = -(-node_sends.shape[0] // LANES) * LANES
    wide = 2 * flow_state.shape[2]
    count, stages, low = 0, 0, 1
    while low < n:
        size = min(group, n // low)
        count, stages, low = count + size - 1, stages + 1, low * size
    hbm = pl.BlockSpec(memory_space=pltpu.HBM)
    constants = [jnp.asarray(t) for t in tables()]
    halo = pltpu.VMEM((5 * FACE, wide), F32)
    place = pltpu.VMEM((8, halo_pad), F32)
    operands = [
        flow_state, state_tangent, far_field.reshape(1, -1), coordinates, damping.reshape(1, -1),
        face_neighbour, element_nodes,
        upper_sends.reshape(1, -1), lower_sends.reshape(1, -1), node_sends.reshape(1, -1),
        shock_flags.reshape(1, -1),
    ] + constants
    shapes = (
        jax.ShapeDtypeStruct(flow_state.shape, F32),
        jax.ShapeDtypeStruct(flow_state.shape, F32),
        jax.ShapeDtypeStruct(coordinates.shape, F32),
    )
    results = pl.pallas_call(
        functools.partial(kernel, n, group),
        out_shape=shapes,
        in_specs=[hbm] * len(operands),
        out_specs=(hbm, hbm, hbm),
        scratch_shapes=[pltpu.VMEM(o.shape, o.dtype) for o in operands + list(shapes)] + [halo] * 4 + [place] * 6 + [
            pltpu.VMEM((stages, 8, LANES), F32),
            pltpu.VMEM((count, 8, LANES), F32),
            pltpu.SemaphoreType.DMA((5 + count,)),
            pltpu.SemaphoreType.DMA((5 + count,)),
            pltpu.SemaphoreType.DMA((INPUTS + 3,)),
        ],
        compiler_params=pltpu.CompilerParams(
            collective_id=0, has_side_effects=True, vmem_limit_bytes=VMEM_LIMIT
        ),
    )(*operands)
    return pl.pallas_call(
        write_out,
        out_shape=shapes,
        in_specs=[hbm] * 3,
        out_specs=[hbm] * 3,
        scratch_shapes=[pltpu.VMEM(o.shape, o.dtype) for o in shapes] + [pltpu.SemaphoreType.DMA((6,))],
        compiler_params=pltpu.CompilerParams(vmem_limit_bytes=VMEM_LIMIT),
    )(*results)


def solution(mesh):
    n = mesh.shape["parts"]
    in_specs = (
        P(None, None, "parts"),
        P(None, None, "parts"),
        P(),
        P(None, "parts"),
        P(),
        P(None, "parts"),
        P(None, "parts"),
        P("parts"),
        P("parts"),
        P("parts"),
        P("parts"),
    )
    out_specs = (P(None, None, "parts"), P(None, None, "parts"), P(None, "parts"))
    return jax.shard_map(
        functools.partial(body, n, 8), mesh=mesh, in_specs=in_specs, out_specs=out_specs,
        check_vma=False,
    )
```
